32 devices in a mesh: grp: 2 (over y), wide: 4 (over z), narrow: 4 (over x, core).
Axes of the slice: x: 2, y: 2, z: 4, core: 2. Of those that a mesh axis runs over, the one named last changes fastest.
Arguments:
- voltages: bfloat16 [8, 256, 81920], P(('grp', 'narrow'), 'wide'), parts along dimension 0, may hold values from -16 to 16
- fir_coeffs: float32 [4, 16384], replicated, may hold values from -0.5 to 3
- channel_keep_flags: int32 [16384], P(('grp', 'wide')), parts along dimension 0, may hold values 0 or 1
Outputs:
- visibilities: bfloat16 [128, 2, 4, 256, 1024], P(('grp', 'wide'), None, 'narrow'), parts along dimension 0
The draws below stay inside these ranges and needn't reach their ends.
There are 2 independent parts, one for each index of `grp`. The reference program is written for one: setup_inputs(seed, part) draws one part's arguments, and reference() takes and returns one part's arrays. A program takes and returns all parts, laid end to end along the dimension named above; an argument that names none is the same for every part. Nothing has to cross between parts.
All inputs are finite; a program needn't handle non-finite values. No bound on the sum of `channel_keep_flags` on one device may be relied on, other than what follows from the above.
Results may differ from the reference program's by a relative error of at most 0.006.
Values may be sent and summed in bfloat16 or wider, within the bound.
A program may use at most 128 MiB of HBM per device.

```python
import jax
import jax.numpy as jnp
from jax import lax

CHANNEL_TOTAL = 8192
TAPS = 4
CHANNELS_PER_BIN = 128
FRAME = 16384
PANELS = 4
PANEL_IN = 256
SAMPLES = 81920


def draw_voltages(key, part):
    noise_key = jax.random.fold_in(key, 11)
    sky_key = jax.random.fold_in(key, 12)
    delay_key = jax.random.fold_in(key, 13)
    gain_key = jax.random.fold_in(key, 14)
    antenna_input_count = PANELS * PANEL_IN
    delay_span = FRAME // 256 + 1
    delays = jax.random.randint(delay_key, (antenna_input_count,), 0, delay_span)
    sky_signal = jnp.clip(jax.random.normal(sky_key, (SAMPLES + delay_span,), jnp.float32), -4.0, 4.0)
    shifted = jax.vmap(lambda delay_start: lax.dynamic_slice(sky_signal, (delay_start,), (SAMPLES,)))(delays)
    noise_part = jnp.clip(jax.random.normal(noise_key, (antenna_input_count, SAMPLES), jnp.float32), -4.0, 4.0)
    input_gain = jax.random.uniform(gain_key, (antenna_input_count, 1), jnp.float32, 0.6, 1.4)
    mixed = noise_part + input_gain * shifted
    return mixed.reshape(PANELS, PANEL_IN, SAMPLES).astype(jnp.bfloat16)


def draw_fir_coeffs(key, part):
    rough_key = jax.random.fold_in(key, 21)
    position = jnp.arange(TAPS * FRAME, dtype=jnp.float32)
    offset = (position + 0.5) / FRAME - TAPS / 2.0
    prototype = jnp.sinc(offset) * (0.5 + 0.5 * jnp.cos(2.0 * jnp.pi * offset / TAPS))
    roughness = jnp.exp(jax.random.uniform(rough_key, (TAPS * FRAME,), jnp.float32, -0.4, 0.4))
    return (prototype * roughness).reshape(TAPS, FRAME)


def place_ends(array, rng, least, top_value):
    shape = array.shape
    spot = [jax.random.randint(jax.random.fold_in(rng, axis), (), 0, shape[axis]) for axis in range(len(shape))]
    array = array.at[tuple(spot)].set(least)
    longest = shape.index(max(shape))
    spot[longest] = (spot[longest] + 1) % shape[longest]
    return array.at[tuple(spot)].set(top_value)


def setup_inputs(seed: int = 0, part: int = 0) -> dict:
    seeds = jax.random.split(jax.random.key(seed), 4)
    part_splits = jax.random.split(jax.random.fold_in(seeds[3], part), 4)
    return {
        "voltages": draw_voltages(jax.random.fold_in(jax.random.fold_in(seeds[3], part), 71), part),
        "fir_coeffs": draw_fir_coeffs(jax.random.fold_in(seeds[3], 71), part),
        "channel_keep_flags": place_ends((jax.random.randint(part_splits[2], (CHANNEL_TOTAL,), 0, 2) < 1).astype(jnp.int32), jax.random.fold_in(part_splits[2], 1), 0, 1),
    }


def reference(voltages, fir_coeffs, channel_keep_flags):
    tap_count, frame_len = fir_coeffs.shape
    panel_total, incoming_panel, sample_total = voltages.shape
    antenna_input_count = panel_total * incoming_panel
    spectrum_count = sample_total // frame_len - tap_count + 1
    per_input = voltages.reshape(antenna_input_count, spectrum_count + tap_count - 1, frame_len)

    def one_input(samples_row):
        filtered = jnp.zeros((spectrum_count, frame_len), jnp.float32)
        for tap_index in range(tap_count):
            filtered = filtered + fir_coeffs[tap_index] * samples_row[tap_index:tap_index + spectrum_count].astype(jnp.float32)
        rounded = lax.optimization_barrier(filtered.astype(jnp.bfloat16))
        spectrum = jnp.fft.rfft(rounded.astype(jnp.float32), axis=-1)[:, :CHANNEL_TOTAL] * (frame_len ** -0.5)
        return jnp.stack([jnp.real(spectrum), jnp.imag(spectrum)]).astype(jnp.bfloat16)

    channel_spectra = lax.map(one_input, per_input)
    output_bin_count = CHANNEL_TOTAL // CHANNELS_PER_BIN
    bin_averaged = channel_spectra.reshape(antenna_input_count, 2, spectrum_count, output_bin_count, CHANNELS_PER_BIN)
    bin_averaged = jnp.transpose(bin_averaged, (3, 1, 0, 2, 4))
    per_bin_masks = channel_keep_flags.reshape(output_bin_count, CHANNELS_PER_BIN).astype(jnp.float32)
    norm_divisor = 1.0 / (spectrum_count * CHANNELS_PER_BIN)

    def one_bin(pair):
        bin_block, bin_mask = pair
        values = bin_block.astype(jnp.float32)
        weighted = values * bin_mask
        high = lax.Precision.HIGHEST
        real_part = jnp.einsum("itk,jtk->ij", weighted[0], values[0], precision=high) + jnp.einsum("itk,jtk->ij", weighted[1], values[1], precision=high)
        imag_part = jnp.einsum("itk,jtk->ij", weighted[1], values[0], precision=high) - jnp.einsum("itk,jtk->ij", weighted[0], values[1], precision=high)
        return (jnp.stack([real_part, imag_part]) * norm_divisor).astype(jnp.bfloat16)

    visibility = lax.map(one_bin, (bin_averaged, per_bin_masks))
    return visibility.reshape(output_bin_count, 2, panel_total, incoming_panel, antenna_input_count)
```

```python
import functools

import jax
import jax.numpy as jnp
import numpy as np
from jax import lax
from jax.experimental import pallas as pl
from jax.experimental.pallas import tpu as pltpu
from jax.sharding import PartitionSpec as P

FACTOR_A = 128


def phase_table(length, outputs, period):
    left_index = jnp.arange(length, dtype=jnp.int32)
    right_index = jnp.arange(outputs, dtype=jnp.int32)
    product = left_index[:, None] * right_index[None, :] % period
    radians = product.astype(jnp.float32) * (2.0 * jnp.pi / period)
    return (jnp.cos(radians), jnp.sin(radians))


def correlate(own_rows, incoming, norm_divisor):
    return (
        jnp.einsum("doqisc,dqmsc->doim", own_rows, incoming, preferred_element_type=jnp.float32)
        * norm_divisor
    )


def plain_body(voltages, fir_coeffs, channel_keep_flags):
    tap_count, frame_len = fir_coeffs.shape
    inputs_here = voltages.shape[1]
    spectrum_count = voltages.shape[2] // frame_len - tap_count + 1
    factor_b = frame_len // FACTOR_A
    blocks = voltages[0].reshape(inputs_here, spectrum_count + tap_count - 1, frame_len)
    filtered = jnp.zeros((inputs_here, spectrum_count, frame_len), jnp.float32)
    for tap_index in range(tap_count):
        filtered = filtered + fir_coeffs[tap_index] * blocks[
            :, tap_index : tap_index + spectrum_count
        ].astype(jnp.float32)
    rounded = lax.optimization_barrier(filtered.astype(jnp.bfloat16))
    folded = rounded.reshape(inputs_here, spectrum_count, FACTOR_A, factor_b)
    high = lax.Precision.HIGHEST
    first_cos, first_sin = phase_table(FACTOR_A, FACTOR_A, FACTOR_A)
    first_table = jnp.stack([first_cos, -first_sin], axis=1)
    table_high = first_table.astype(jnp.bfloat16)
    table_low = (first_table - table_high.astype(jnp.float32)).astype(jnp.bfloat16)
    first_pass = jnp.einsum(
        "psab,aqc->psbqc", folded, table_high, preferred_element_type=jnp.float32
    )
    first_pass = first_pass + jnp.einsum(
        "psab,aqc->psbqc", folded, table_low, preferred_element_type=jnp.float32
    )
    twist_cos, twist_sin = phase_table(factor_b, FACTOR_A, frame_len)
    real_part = first_pass[:, :, :, 0] * twist_cos + first_pass[:, :, :, 1] * twist_sin
    imag_part = first_pass[:, :, :, 1] * twist_cos - first_pass[:, :, :, 0] * twist_sin
    twisted = jnp.stack([real_part, imag_part], axis=3)
    last_cos, last_sin = phase_table(factor_b, factor_b // 2, factor_b)
    cos_rows = last_cos.T
    sin_rows = last_sin.T
    last_table = jnp.stack(
        [jnp.stack([cos_rows, sin_rows], axis=1), jnp.stack([-sin_rows, cos_rows], axis=1)], axis=1
    )
    channel_spectra = jnp.einsum("dqrb,psbrc->dqpsc", last_table, twisted, precision=high)
    channel_spectra = (channel_spectra * frame_len ** (-0.5)).astype(jnp.bfloat16)
    turned = lax.all_to_all(channel_spectra, "wide", split_axis=0, concat_axis=2, tiled=True)
    local_bins = turned.shape[0]
    bin_width = turned.shape[4]
    flag_block = channel_keep_flags.astype(jnp.bfloat16).reshape(local_bins, 1, 1, 1, bin_width)
    weighted = turned * flag_block
    rotated = jnp.stack([weighted[:, 1], -weighted[:, 0]], axis=1)
    own_rows = jnp.stack([weighted, rotated], axis=1)
    norm_divisor = 1.0 / (spectrum_count * bin_width)
    gathered = correlate(
        own_rows, lax.all_gather(turned, "narrow", axis=2, tiled=True), norm_divisor
    )
    result = gathered.astype(jnp.bfloat16)
    return result[:, :, None]


ROWS = 16


def split_table(table):
    high = table.astype(jnp.bfloat16)
    low = (table - high.astype(np.float64)).astype(jnp.bfloat16)
    return high, low


def dft_tables(frame_len):
    side = FACTOR_A
    index = np.arange(side)
    turn = 2.0 * np.pi * (np.outer(index, index) % side) / side
    first = np.concatenate([np.cos(turn), -np.sin(turn)], axis=0)
    first = np.concatenate(split_table(first), axis=1)
    twist = 2.0 * np.pi * np.outer(index, index) / frame_len
    twist = np.stack([np.cos(twist), np.sin(twist)]).astype(np.float32)
    last_cos, last_sin = np.cos(turn[: side // 2]), np.sin(turn[: side // 2])
    real_row = np.concatenate([last_cos, last_sin], axis=1)
    imag_row = np.concatenate([-last_sin, last_cos], axis=1)
    last = np.stack([real_row, imag_row], axis=1).reshape(side, 2 * side)
    last = last * frame_len ** (-0.5)
    last = np.concatenate(split_table(last), axis=0)
    return first, twist, last


def dft_rows(spectra_in, row, first_ref, twist_ref, last_ref, flip):
    side = FACTOR_A
    samples = jnp.concatenate([ref[row] for ref in spectra_in], axis=1)
    samples = jnp.concatenate([samples, samples], axis=0)
    first_pass = jnp.dot(first_ref[...], samples, preferred_element_type=jnp.float32)
    twisted = []
    for s in range(len(spectra_in)):
        real = first_pass[:side, s * side : (s + 1) * side]
        imag = first_pass[side:, s * side : (s + 1) * side]
        cos, sin = twist_ref[0], twist_ref[1]
        twisted.append(
            jnp.concatenate([real * cos + imag * sin, imag * cos - real * sin], axis=1)
        )
    twisted = jnp.concatenate(twisted, axis=0).astype(jnp.bfloat16)
    both = lax.dot_general(
        last_ref[...], twisted, (((1,), (1,)), ((), ())), preferred_element_type=jnp.float32
    )
    total = both[:side] + both[side:]
    start = pl.multiple_of(lax.rem(row, ROWS) * side, side)
    for s in range(len(spectra_in)):
        flip[s, pl.ds(start, side), :] = total[:, s * side : (s + 1) * side]


def dft_kernel(x0_ref, x1_ref, first_ref, twist_ref, last_ref, out_ref, flip):
    side = FACTOR_A

    def one(row, carry):
        dft_rows((x0_ref, x1_ref), row, first_ref, twist_ref, last_ref, flip)
        return carry

    lax.fori_loop(0, ROWS, one, 0, unroll=4)
    for dq in range(side):
        for s in range(2):
            out_ref[dq, :, s * side : (s + 1) * side] = flip[
                s, pl.ds(dq, ROWS, stride=side), :
            ].astype(jnp.bfloat16)


def dft(blocks, frame_len):
    first, twist, last = dft_tables(frame_len)
    rows, side = blocks[0].shape[0], FACTOR_A
    whole = lambda *shape: pl.BlockSpec(shape, lambda i: (0,) * len(shape))
    return pl.pallas_call(
        dft_kernel,
        grid=(rows // ROWS,),
        in_specs=[pl.BlockSpec((ROWS, side, side), lambda i: (i, 0, 0))] * 2
        + [whole(2 * side, 2 * side), whole(2, side, side), whole(2 * side, 2 * side)],
        out_specs=pl.BlockSpec((side, ROWS, 2 * side), lambda i: (0, i, 0)),
        out_shape=jax.ShapeDtypeStruct((side, rows, 2 * side), jnp.bfloat16),
        scratch_shapes=[pltpu.VMEM((2, ROWS * side, side), jnp.float32)],
        compiler_params=pltpu.CompilerParams(vmem_limit_bytes=40 * 2**20),
    )(*blocks, jnp.asarray(first), jnp.asarray(twist), jnp.asarray(last))


def correlate_kernel(scale, rows, flag_ref, all_ref, out_ref):
    start = pl.multiple_of(lax.axis_index("narrow") * rows, rows)
    flags = flag_ref[0]
    own_real = all_ref[0, 0, pl.ds(start, rows), :] * flags
    own_imag = all_ref[0, 1, pl.ds(start, rows), :] * flags
    columns = jnp.concatenate([all_ref[0, 0], all_ref[0, 1]], axis=1)
    for part, own in enumerate(((own_real, own_imag), (own_imag, -own_real))):
        total = lax.dot_general(
            jnp.concatenate(own, axis=1),
            columns,
            (((1,), (1,)), ((), ())),
            preferred_element_type=jnp.float32,
        )
        out_ref[0, part, 0] = (total * scale).astype(jnp.bfloat16)


def correlate_bins(gathered, flags, rows, scale):
    bins, parts, inputs, depth = gathered.shape
    return pl.pallas_call(
        functools.partial(correlate_kernel, scale, rows),
        grid=(bins,),
        in_specs=[
            pl.BlockSpec((1, 1, depth), lambda b: (b, 0, 0)),
            pl.BlockSpec((1, parts, inputs, depth), lambda b: (b, 0, 0, 0)),
        ],
        out_specs=pl.BlockSpec((1, parts, 1, rows, inputs), lambda b: (b, 0, 0, 0, 0)),
        out_shape=jax.ShapeDtypeStruct((bins, parts, 1, rows, inputs), jnp.bfloat16),
        compiler_params=pltpu.CompilerParams(vmem_limit_bytes=40 * 2**20),
    )(flags, gathered)


def filter_rows(voltages, fir_coeffs, spectrum):
    frame_len = fir_coeffs.shape[1]
    total = 0.0
    for tap_index in range(fir_coeffs.shape[0]):
        start = (spectrum + tap_index) * frame_len
        block = voltages[:, start : start + frame_len].astype(jnp.float32)
        total = total + fir_coeffs[tap_index] * block
    return total.astype(jnp.bfloat16)


def fast_body(wide, voltages, fir_coeffs, channel_keep_flags):
    tap_count, frame_len = fir_coeffs.shape
    inputs_here = voltages.shape[1]
    spectrum_count = voltages.shape[2] // frame_len - tap_count + 1
    bin_width = FACTOR_A
    local_bins = channel_keep_flags.shape[0] // bin_width
    filtered = [filter_rows(voltages[0], fir_coeffs, s) for s in range(spectrum_count)]
    blocks = [lax.optimization_barrier(x).reshape(inputs_here, FACTOR_A, FACTOR_A) for x in filtered]
    spectra = dft(blocks, frame_len).reshape(wide * local_bins, 2, inputs_here, 2 * bin_width)
    turned = lax.all_to_all(spectra, "wide", split_axis=0, concat_axis=2, tiled=True)
    gathered = lax.all_gather(turned, "narrow", axis=2, tiled=True)
    flags = channel_keep_flags.astype(jnp.bfloat16).reshape(local_bins, 1, bin_width)
    flags = jnp.concatenate([flags] * spectrum_count, axis=2)
    scale = 1.0 / (spectrum_count * bin_width)
    return correlate_bins(gathered, flags, wide * inputs_here, scale)


def solution(mesh):
    wide = mesh.shape["wide"]
    narrow = mesh.shape["narrow"]

    def body(voltages, fir_coeffs, channel_keep_flags):
        tap_count, frame_len = fir_coeffs.shape
        rows = voltages.shape[1]
        spectrum_count = voltages.shape[2] // frame_len - tap_count + 1
        fits = frame_len == FACTOR_A**2 and rows % ROWS == 0 and spectrum_count == 2
        if fits and narrow == 4:
            return fast_body(wide, voltages, fir_coeffs, channel_keep_flags)
        return plain_body(voltages, fir_coeffs, channel_keep_flags)

    placed = (P(("grp", "narrow"), "wide", None), P(), P(("grp", "wide")))
    return jax.shard_map(
        body,
        mesh=mesh,
        in_specs=placed,
        out_specs=P(("grp", "wide"), None, "narrow", None, None),
        check_vma=False,
    )
```

```python
import functools

import jax
import jax.numpy as jnp
import numpy as np
from jax import lax
from jax.experimental import pallas as pl
from jax.experimental.pallas import tpu as pltpu
from jax.sharding import PartitionSpec as P

FACTOR_A = 128


def phase_table(length, outputs, period):
    left_index = jnp.arange(length, dtype=jnp.int32)
    right_index = jnp.arange(outputs, dtype=jnp.int32)
    product = left_index[:, None] * right_index[None, :] % period
    radians = product.astype(jnp.float32) * (2.0 * jnp.pi / period)
    return (jnp.cos(radians), jnp.sin(radians))


def correlate(own_rows, incoming, norm_divisor):
    return (
        jnp.einsum("doqisc,dqmsc->doim", own_rows, incoming, preferred_element_type=jnp.float32)
        * norm_divisor
    )


def plain_body(voltages, fir_coeffs, channel_keep_flags):
    tap_count, frame_len = fir_coeffs.shape
    inputs_here = voltages.shape[1]
    spectrum_count = voltages.shape[2] // frame_len - tap_count + 1
    factor_b = frame_len // FACTOR_A
    blocks = voltages[0].reshape(inputs_here, spectrum_count + tap_count - 1, frame_len)
    filtered = jnp.zeros((inputs_here, spectrum_count, frame_len), jnp.float32)
    for tap_index in range(tap_count):
        filtered = filtered + fir_coeffs[tap_index] * blocks[
            :, tap_index : tap_index + spectrum_count
        ].astype(jnp.float32)
    rounded = lax.optimization_barrier(filtered.astype(jnp.bfloat16))
    folded = rounded.reshape(inputs_here, spectrum_count, FACTOR_A, factor_b)
    high = lax.Precision.HIGHEST
    first_cos, first_sin = phase_table(FACTOR_A, FACTOR_A, FACTOR_A)
    first_table = jnp.stack([first_cos, -first_sin], axis=1)
    table_high = first_table.astype(jnp.bfloat16)
    table_low = (first_table - table_high.astype(jnp.float32)).astype(jnp.bfloat16)
    first_pass = jnp.einsum(
        "psab,aqc->psbqc", folded, table_high, preferred_element_type=jnp.float32
    )
    first_pass = first_pass + jnp.einsum(
        "psab,aqc->psbqc", folded, table_low, preferred_element_type=jnp.float32
    )
    twist_cos, twist_sin = phase_table(factor_b, FACTOR_A, frame_len)
    real_part = first_pass[:, :, :, 0] * twist_cos + first_pass[:, :, :, 1] * twist_sin
    imag_part = first_pass[:, :, :, 1] * twist_cos - first_pass[:, :, :, 0] * twist_sin
    twisted = jnp.stack([real_part, imag_part], axis=3)
    last_cos, last_sin = phase_table(factor_b, factor_b // 2, factor_b)
    cos_rows = last_cos.T
    sin_rows = last_sin.T
    last_table = jnp.stack(
        [jnp.stack([cos_rows, sin_rows], axis=1), jnp.stack([-sin_rows, cos_rows], axis=1)], axis=1
    )
    channel_spectra = jnp.einsum("dqrb,psbrc->dqpsc", last_table, twisted, precision=high)
    channel_spectra = (channel_spectra * frame_len ** (-0.5)).astype(jnp.bfloat16)
    turned = lax.all_to_all(channel_spectra, "wide", split_axis=0, concat_axis=2, tiled=True)
    local_bins = turned.shape[0]
    bin_width = turned.shape[4]
    flag_block = channel_keep_flags.astype(jnp.bfloat16).reshape(local_bins, 1, 1, 1, bin_width)
    weighted = turned * flag_block
    rotated = jnp.stack([weighted[:, 1], -weighted[:, 0]], axis=1)
    own_rows = jnp.stack([weighted, rotated], axis=1)
    norm_divisor = 1.0 / (spectrum_count * bin_width)
    gathered = correlate(
        own_rows, lax.all_gather(turned, "narrow", axis=2, tiled=True), norm_divisor
    )
    result = gathered.astype(jnp.bfloat16)
    return result[:, :, None]


ROWS = 16
CHUNKS = 8
ORDER = (2, 1, 3)


def split_table(table):
    high = table.astype(jnp.bfloat16)
    low = (table - high.astype(np.float64)).astype(jnp.bfloat16)
    return high, low


def dft_tables(frame_len):
    side = FACTOR_A
    index = np.arange(side)
    turn = 2.0 * np.pi * (np.outer(index, index) % side) / side
    first = np.concatenate([np.cos(turn), -np.sin(turn)], axis=0)
    first = np.concatenate(split_table(first), axis=1)
    twist = 2.0 * np.pi * np.outer(index, index) / frame_len
    twist = np.stack([np.cos(twist), np.sin(twist)]).astype(np.float32)
    last_cos, last_sin = np.cos(turn[: side // 2]), np.sin(turn[: side // 2])
    real_row = np.concatenate([last_cos, last_sin], axis=1)
    imag_row = np.concatenate([-last_sin, last_cos], axis=1)
    last = np.stack([real_row, imag_row], axis=1).reshape(side, 2 * side)
    last = last * frame_len ** (-0.5)
    last = np.concatenate(split_table(last), axis=0)
    return first, twist, last


def dft_rows(spectra_in, row, first_ref, twist_ref, last_ref, flip):
    side = FACTOR_A
    samples = jnp.concatenate([ref[row] for ref in spectra_in], axis=1)
    samples = jnp.concatenate([samples, samples], axis=0)
    first_pass = jnp.dot(first_ref[...], samples, preferred_element_type=jnp.float32)
    twisted = []
    for s in range(len(spectra_in)):
        real = first_pass[:side, s * side : (s + 1) * side]
        imag = first_pass[side:, s * side : (s + 1) * side]
        cos, sin = twist_ref[0], twist_ref[1]
        twisted.append(
            jnp.concatenate([real * cos + imag * sin, imag * cos - real * sin], axis=1)
        )
    twisted = jnp.concatenate(twisted, axis=0).astype(jnp.bfloat16)
    both = lax.dot_general(
        last_ref[...], twisted, (((1,), (1,)), ((), ())), preferred_element_type=jnp.float32
    )
    total = both[:side] + both[side:]
    start = pl.multiple_of(lax.rem(row, ROWS) * side, side)
    for s in range(len(spectra_in)):
        flip[s, pl.ds(start, side), :] = total[:, s * side : (s + 1) * side]


def dft_kernel(x0_ref, x1_ref, first_ref, twist_ref, last_ref, out_ref, flip):
    side = FACTOR_A

    def one(row, carry):
        dft_rows((x0_ref, x1_ref), row, first_ref, twist_ref, last_ref, flip)
        return carry

    lax.fori_loop(0, ROWS, one, 0, unroll=4)
    for dq in range(side):
        for s in range(2):
            out_ref[dq, :, s * side : (s + 1) * side] = flip[
                s, pl.ds(dq, ROWS, stride=side), :
            ].astype(jnp.bfloat16)


def dft(blocks, frame_len):
    first, twist, last = dft_tables(frame_len)
    rows, side = blocks[0].shape[0], FACTOR_A
    whole = lambda *shape: pl.BlockSpec(shape, lambda i: (0,) * len(shape))
    return pl.pallas_call(
        dft_kernel,
        grid=(rows // ROWS,),
        in_specs=[pl.BlockSpec((ROWS, side, side), lambda i: (i, 0, 0))] * 2
        + [whole(2 * side, 2 * side), whole(2, side, side), whole(2 * side, 2 * side)],
        out_specs=pl.BlockSpec((side, ROWS, 2 * side), lambda i: (0, i, 0)),
        out_shape=jax.ShapeDtypeStruct((side, rows, 2 * side), jnp.bfloat16),
        scratch_shapes=[pltpu.VMEM((2, ROWS * side, side), jnp.float32)],
        compiler_params=pltpu.CompilerParams(vmem_limit_bytes=40 * 2**20),
    )(*blocks, jnp.asarray(first), jnp.asarray(twist), jnp.asarray(last))


def correlate_kernel(scale, rows, flag_ref, all_ref, out_ref):
    start = pl.multiple_of(lax.axis_index("narrow") * rows, rows)
    flags = flag_ref[0]
    own_real = all_ref[0, 0, pl.ds(start, rows), :] * flags
    own_imag = all_ref[0, 1, pl.ds(start, rows), :] * flags
    columns = jnp.concatenate([all_ref[0, 0], all_ref[0, 1]], axis=1)
    for part, own in enumerate(((own_real, own_imag), (own_imag, -own_real))):
        total = lax.dot_general(
            jnp.concatenate(own, axis=1),
            columns,
            (((1,), (1,)), ((), ())),
            preferred_element_type=jnp.float32,
        )
        out_ref[0, part, 0] = (total * scale).astype(jnp.bfloat16)


def correlate_bins(gathered, flags, rows, scale):
    bins, parts, inputs, depth = gathered.shape
    return pl.pallas_call(
        functools.partial(correlate_kernel, scale, rows),
        grid=(bins,),
        in_specs=[
            pl.BlockSpec((1, 1, depth), lambda b: (b, 0, 0)),
            pl.BlockSpec((1, parts, inputs, depth), lambda b: (b, 0, 0, 0)),
        ],
        out_specs=pl.BlockSpec((1, parts, 1, rows, inputs), lambda b: (b, 0, 0, 0, 0)),
        out_shape=jax.ShapeDtypeStruct((bins, parts, 1, rows, inputs), jnp.bfloat16),
        compiler_params=pltpu.CompilerParams(vmem_limit_bytes=40 * 2**20),
    )(flags, gathered)


def move_kernel(wide, chunks, spectra, gathered, local_sem, z_send, z_recv, x_send, x_recv,
                pair_send, pair_recv, last_send, last_recv):
    me = lax.axis_index("wide")
    panel = lax.axis_index("narrow")
    pair = panel + 1 - 2 * lax.rem(panel, 2)
    across = lax.rem(panel + 2, 4)
    across_pair = lax.rem(pair + 2, 4)
    rows = spectra.shape[3]
    size = spectra.shape[1] // chunks

    barrier = pltpu.get_barrier_semaphore()
    peers = [{"wide": lax.rem(me + step, wide)} for step in range(1, wide)]
    peers += [{"narrow": pair}, {"narrow": across}]
    for peer in peers:
        pl.semaphore_signal(barrier, inc=1, device_id=peer, device_id_type=pl.DeviceIdType.MESH)
    pl.semaphore_wait(barrier, len(peers))

    def spot(chunk, owner, source):
        start = pl.multiple_of((owner * wide + source) * rows, rows)
        return gathered.at[pl.ds(chunk * size, size), :, pl.ds(start, rows), :]

    def mine(target, chunk):
        return spectra.at[target, pl.ds(chunk * size, size)]

    def remote(src, dst, send, recv, peer):
        return pltpu.make_async_remote_copy(
            src_ref=src, dst_ref=dst, send_sem=send, recv_sem=recv,
            device_id=peer, device_id_type=pl.DeviceIdType.MESH,
        )

    def along(chunk, step):
        target = lax.rem(me + step, wide)
        return remote(mine(target, chunk), spot(chunk, panel, me), z_send.at[chunk, step],
                      z_recv.at[chunk, step], {"wide": target})

    def arriving(chunk, step):
        source = lax.rem(me + wide - step, wide)
        return remote(mine(me, chunk), spot(chunk, panel, source), z_send.at[chunk, step],
                      z_recv.at[chunk, step], {"wide": source})

    def block_at(chunk, step, owner):
        return spot(chunk, owner, lax.rem(me + wide - step, wide))

    def first_hop(chunk, step, to_pair, receiving=False):
        owner = (pair if to_pair else across) if receiving else panel
        dst = block_at(chunk, step, owner)
        src = mine(me, chunk) if step == 0 else block_at(chunk, step, panel)
        send, recv = (pair_send, pair_recv) if to_pair else (x_send, x_recv)
        return remote(src, dst, send.at[chunk, step], recv.at[chunk, step],
                      {"narrow": pair if to_pair else across})

    def second_hop(chunk, step, receiving=False):
        block = block_at(chunk, step, across_pair if receiving else across)
        return remote(block, block, last_send.at[chunk, step], last_recv.at[chunk, step],
                      {"narrow": pair})

    def begin(chunk, carry):
        first_hop(chunk, 0, False).start()
        for step in ORDER:
            along(chunk, step).start()
        first_hop(chunk, 0, True).start()
        pltpu.make_async_copy(mine(me, chunk), spot(chunk, panel, me), local_sem.at[chunk]).start()
        return carry

    def onward(chunk, carry):
        for step in range(1, wide):
            arriving(chunk, step).wait_recv()
            first_hop(chunk, step, False).start()
            first_hop(chunk, step, True).start()
        return carry

    def relay(chunk, carry):
        for step in range(wide):
            first_hop(chunk, step, False, True).wait_recv()
            second_hop(chunk, step).start()
        return carry

    def both(chunk, carry):
        onward(chunk, carry)
        relay(chunk - 1, carry)
        return carry

    def finish(chunk, carry):
        pltpu.make_async_copy(mine(me, chunk), spot(chunk, panel, me), local_sem.at[chunk]).wait()
        for step in range(wide):
            if step > 0:
                along(chunk, step).wait_send()
            first_hop(chunk, step, False).wait_send()
            first_hop(chunk, step, True).wait_send()
            first_hop(chunk, step, True, True).wait_recv()
            second_hop(chunk, step).wait_send()
            second_hop(chunk, step, True).wait_recv()
        return carry

    lax.fori_loop(0, chunks, begin, 0)
    onward(0, 0)
    lax.fori_loop(1, chunks, both, 0)
    relay(chunks - 1, 0)
    lax.fori_loop(0, chunks, finish, 0)


def move(spectra, wide, narrow):
    bins, parts, rows, depth = spectra.shape[1:]
    chunks = CHUNKS
    table = pltpu.SemaphoreType.DMA((chunks, wide))
    return pl.pallas_call(
        functools.partial(move_kernel, wide, chunks),
        in_specs=[pl.BlockSpec(memory_space=pl.ANY)],
        out_specs=pl.BlockSpec(memory_space=pl.ANY),
        out_shape=jax.ShapeDtypeStruct((bins, parts, narrow * wide * rows, depth), jnp.bfloat16),
        scratch_shapes=[pltpu.SemaphoreType.DMA((chunks,))] + [table] * 8,
        compiler_params=pltpu.CompilerParams(collective_id=0, has_side_effects=True),
    )(spectra)


def filter_rows(voltages, fir_coeffs, spectrum):
    frame_len = fir_coeffs.shape[1]
    total = 0.0
    for tap_index in range(fir_coeffs.shape[0]):
        start = (spectrum + tap_index) * frame_len
        block = voltages[:, start : start + frame_len].astype(jnp.float32)
        total = total + fir_coeffs[tap_index] * block
    return total.astype(jnp.bfloat16)


def fast_body(wide, voltages, fir_coeffs, channel_keep_flags):
    tap_count, frame_len = fir_coeffs.shape
    inputs_here = voltages.shape[1]
    spectrum_count = voltages.shape[2] // frame_len - tap_count + 1
    bin_width = FACTOR_A
    local_bins = channel_keep_flags.shape[0] // bin_width
    filtered = [filter_rows(voltages[0], fir_coeffs, s) for s in range(spectrum_count)]
    blocks = [lax.optimization_barrier(x).reshape(inputs_here, FACTOR_A, FACTOR_A) for x in filtered]
    spectra = dft(blocks, frame_len).reshape(wide, local_bins, 2, inputs_here, 2 * bin_width)
    gathered = move(spectra, wide, 4)
    flags = channel_keep_flags.astype(jnp.bfloat16).reshape(local_bins, 1, bin_width)
    flags = jnp.concatenate([flags] * spectrum_count, axis=2)
    scale = 1.0 / (spectrum_count * bin_width)
    return correlate_bins(gathered, flags, wide * inputs_here, scale)


def solution(mesh):
    wide = mesh.shape["wide"]
    narrow = mesh.shape["narrow"]

    def body(voltages, fir_coeffs, channel_keep_flags):
        tap_count, frame_len = fir_coeffs.shape
        rows = voltages.shape[1]
        spectrum_count = voltages.shape[2] // frame_len - tap_count + 1
        fits = frame_len == FACTOR_A**2 and rows % ROWS == 0 and spectrum_count == 2
        bins_fit = channel_keep_flags.shape[0] // FACTOR_A % CHUNKS == 0
        if fits and bins_fit and narrow == 4 and wide == 4:
            return fast_body(wide, voltages, fir_coeffs, channel_keep_flags)
        return plain_body(voltages, fir_coeffs, channel_keep_flags)

    placed = (P(("grp", "narrow"), "wide", None), P(), P(("grp", "wide")))
    return jax.shard_map(
        body,
        mesh=mesh,
        in_specs=placed,
        out_specs=P(("grp", "wide"), None, "narrow", None, None),
        check_vma=False,
    )
```

```python
import functools

import jax
import jax.numpy as jnp
import numpy as np
from jax import lax
from jax.experimental import pallas as pl
from jax.experimental.pallas import tpu as pltpu
from jax.sharding import PartitionSpec as P

FACTOR_A = 128


def phase_table(length, outputs, period):
    left_index = jnp.arange(length, dtype=jnp.int32)
    right_index = jnp.arange(outputs, dtype=jnp.int32)
    product = left_index[:, None] * right_index[None, :] % period
    radians = product.astype(jnp.float32) * (2.0 * jnp.pi / period)
    return (jnp.cos(radians), jnp.sin(radians))


def correlate(own_rows, incoming, norm_divisor):
    return (
        jnp.einsum("doqisc,dqmsc->doim", own_rows, incoming, preferred_element_type=jnp.float32)
        * norm_divisor
    )


def plain_body(voltages, fir_coeffs, channel_keep_flags):
    tap_count, frame_len = fir_coeffs.shape
    inputs_here = voltages.shape[1]
    spectrum_count = voltages.shape[2] // frame_len - tap_count + 1
    factor_b = frame_len // FACTOR_A
    blocks = voltages[0].reshape(inputs_here, spectrum_count + tap_count - 1, frame_len)
    filtered = jnp.zeros((inputs_here, spectrum_count, frame_len), jnp.float32)
    for tap_index in range(tap_count):
        filtered = filtered + fir_coeffs[tap_index] * blocks[
            :, tap_index : tap_index + spectrum_count
        ].astype(jnp.float32)
    rounded = lax.optimization_barrier(filtered.astype(jnp.bfloat16))
    folded = rounded.reshape(inputs_here, spectrum_count, FACTOR_A, factor_b)
    high = lax.Precision.HIGHEST
    first_cos, first_sin = phase_table(FACTOR_A, FACTOR_A, FACTOR_A)
    first_table = jnp.stack([first_cos, -first_sin], axis=1)
    table_high = first_table.astype(jnp.bfloat16)
    table_low = (first_table - table_high.astype(jnp.float32)).astype(jnp.bfloat16)
    first_pass = jnp.einsum(
        "psab,aqc->psbqc", folded, table_high, preferred_element_type=jnp.float32
    )
    first_pass = first_pass + jnp.einsum(
        "psab,aqc->psbqc", folded, table_low, preferred_element_type=jnp.float32
    )
    twist_cos, twist_sin = phase_table(factor_b, FACTOR_A, frame_len)
    real_part = first_pass[:, :, :, 0] * twist_cos + first_pass[:, :, :, 1] * twist_sin
    imag_part = first_pass[:, :, :, 1] * twist_cos - first_pass[:, :, :, 0] * twist_sin
    twisted = jnp.stack([real_part, imag_part], axis=3)
    last_cos, last_sin = phase_table(factor_b, factor_b // 2, factor_b)
    cos_rows = last_cos.T
    sin_rows = last_sin.T
    last_table = jnp.stack(
        [jnp.stack([cos_rows, sin_rows], axis=1), jnp.stack([-sin_rows, cos_rows], axis=1)], axis=1
    )
    channel_spectra = jnp.einsum("dqrb,psbrc->dqpsc", last_table, twisted, precision=high)
    channel_spectra = (channel_spectra * frame_len ** (-0.5)).astype(jnp.bfloat16)
    turned = lax.all_to_all(channel_spectra, "wide", split_axis=0, concat_axis=2, tiled=True)
    local_bins = turned.shape[0]
    bin_width = turned.shape[4]
    flag_block = channel_keep_flags.astype(jnp.bfloat16).reshape(local_bins, 1, 1, 1, bin_width)
    weighted = turned * flag_block
    rotated = jnp.stack([weighted[:, 1], -weighted[:, 0]], axis=1)
    own_rows = jnp.stack([weighted, rotated], axis=1)
    norm_divisor = 1.0 / (spectrum_count * bin_width)
    gathered = correlate(
        own_rows, lax.all_gather(turned, "narrow", axis=2, tiled=True), norm_divisor
    )
    result = gathered.astype(jnp.bfloat16)
    return result[:, :, None]


ROWS = 16
GROUPS = 4
ORDER = (2, 1, 3)


def split_table(table):
    high = table.astype(jnp.bfloat16)
    low = (table - high.astype(np.float64)).astype(jnp.bfloat16)
    return high, low


def dft_tables(frame_len):
    side = FACTOR_A
    index = np.arange(side)
    turn = 2.0 * np.pi * (np.outer(index, index) % side) / side
    first = np.concatenate([np.cos(turn), -np.sin(turn)], axis=0)
    first = np.concatenate(split_table(first), axis=1)
    twist = 2.0 * np.pi * np.outer(index, index) / frame_len
    twist = np.stack([np.cos(twist), np.sin(twist)]).astype(np.float32)
    last_cos, last_sin = np.cos(turn[: side // 2]), np.sin(turn[: side // 2])
    real_row = np.concatenate([last_cos, last_sin], axis=1)
    imag_row = np.concatenate([-last_sin, last_cos], axis=1)
    last = np.stack([real_row, imag_row], axis=1).reshape(side, 2 * side)
    last = last * frame_len ** (-0.5)
    last = np.concatenate(split_table(last), axis=0)
    return first, twist, last


def dft_rows(spectra_in, row, first_ref, twist_ref, last_ref, flip):
    side = FACTOR_A
    samples = jnp.concatenate([ref[row] for ref in spectra_in], axis=1)
    samples = jnp.concatenate([samples, samples], axis=0)
    first_pass = jnp.dot(first_ref[...], samples, preferred_element_type=jnp.float32)
    twisted = []
    for s in range(len(spectra_in)):
        real = first_pass[:side, s * side : (s + 1) * side]
        imag = first_pass[side:, s * side : (s + 1) * side]
        cos, sin = twist_ref[0], twist_ref[1]
        twisted.append(
            jnp.concatenate([real * cos + imag * sin, imag * cos - real * sin], axis=1)
        )
    twisted = jnp.concatenate(twisted, axis=0).astype(jnp.bfloat16)
    both = lax.dot_general(
        last_ref[...], twisted, (((1,), (1,)), ((), ())), preferred_element_type=jnp.float32
    )
    total = both[:side] + both[side:]
    start = pl.multiple_of(lax.rem(row, ROWS) * side, side)
    for s in range(len(spectra_in)):
        flip[s, pl.ds(start, side), :] = total[:, s * side : (s + 1) * side]


def dft_chunk(spectra_in, chunk, tables, flip, spectra):
    side = FACTOR_A
    _, wide, bins, parts, _, _ = spectra.shape

    def one(row, carry):
        dft_rows(spectra_in, chunk * ROWS + row, *tables, flip)
        return carry

    lax.fori_loop(0, ROWS, one, 0, unroll=4)
    for dq in range(side):
        target, bin_index, part = dq // (bins * parts), dq // parts % bins, dq % parts
        for s in range(len(spectra_in)):
            spectra[chunk, target, bin_index, part, :, s * side : (s + 1) * side] = flip[
                s, pl.ds(dq, ROWS, stride=side), :
            ].astype(jnp.bfloat16)


def correlate_kernel(scale, rows, flag_ref, all_ref, out_ref):
    start = pl.multiple_of(lax.axis_index("narrow") * rows, rows)
    flags = flag_ref[0]
    own_real = all_ref[0, 0, pl.ds(start, rows), :] * flags
    own_imag = all_ref[0, 1, pl.ds(start, rows), :] * flags
    columns = jnp.concatenate([all_ref[0, 0], all_ref[0, 1]], axis=1)
    own = jnp.concatenate(
        [
            jnp.concatenate([own_real, own_imag], axis=1),
            jnp.concatenate([own_imag, -own_real], axis=1),
        ],
        axis=0,
    )
    total = lax.dot_general(
        own, columns, (((1,), (1,)), ((), ())), preferred_element_type=jnp.float32
    )
    total = (total * scale).astype(jnp.bfloat16)
    out_ref[0, 0, 0] = total[:rows]
    out_ref[0, 1, 0] = total[rows:]


def correlate_bins(gathered, flags, rows, scale):
    bins, parts, inputs, depth = gathered.shape
    return pl.pallas_call(
        functools.partial(correlate_kernel, scale, rows),
        grid=(bins,),
        in_specs=[
            pl.BlockSpec((1, 1, depth), lambda b: (b, 0, 0)),
            pl.BlockSpec((1, parts, inputs, depth), lambda b: (b, 0, 0, 0)),
        ],
        out_specs=pl.BlockSpec((1, parts, 1, rows, inputs), lambda b: (b, 0, 0, 0, 0)),
        out_shape=jax.ShapeDtypeStruct((bins, parts, 1, rows, inputs), jnp.bfloat16),
        compiler_params=pltpu.CompilerParams(vmem_limit_bytes=40 * 2**20),
    )(flags, gathered)


def move_kernel(wide, x0_ref, x1_ref, first_ref, twist_ref, last_ref, gathered, flip, spectra,
                local_sem, z_send, z_recv, x_send, x_recv, pair_send, pair_recv, last_send,
                last_recv):
    me = lax.axis_index("wide")
    panel = lax.axis_index("narrow")
    pair = panel + 1 - 2 * lax.rem(panel, 2)
    across = lax.rem(panel + 2, 4)
    across_pair = lax.rem(pair + 2, 4)
    rows = x0_ref.shape[0]
    row_chunks = rows // ROWS
    chunks = row_chunks * GROUPS
    size = spectra.shape[2] // GROUPS

    barrier = pltpu.get_barrier_semaphore()
    peers = [{"wide": lax.rem(me + step, wide)} for step in range(1, wide)]
    peers += [{"narrow": pair}, {"narrow": across}]
    for peer in peers:
        pl.semaphore_signal(barrier, inc=1, device_id=peer, device_id_type=pl.DeviceIdType.MESH)
    pl.semaphore_wait(barrier, len(peers))

    def spot(chunk, owner, source):
        start = (owner * wide + source) * rows + chunk // GROUPS * ROWS
        group = chunk % GROUPS
        start = pl.multiple_of(start, ROWS)
        return gathered.at[pl.ds(group * size, size), :, pl.ds(start, ROWS), :]

    def mine(target, chunk):
        group = chunk % GROUPS
        return spectra.at[chunk // GROUPS, target, pl.ds(group * size, size)]

    def remote(src, dst, send, recv, peer):
        return pltpu.make_async_remote_copy(
            src_ref=src, dst_ref=dst, send_sem=send, recv_sem=recv,
            device_id=peer, device_id_type=pl.DeviceIdType.MESH,
        )

    def along(chunk, step):
        target = lax.rem(me + step, wide)
        return remote(mine(target, chunk), spot(chunk, panel, me), z_send.at[chunk, step],
                      z_recv.at[chunk, step], {"wide": target})

    def arriving(chunk, step):
        source = lax.rem(me + wide - step, wide)
        return remote(mine(me, chunk), spot(chunk, panel, source), z_send.at[chunk, step],
                      z_recv.at[chunk, step], {"wide": source})

    def block_at(chunk, step, owner):
        return spot(chunk, owner, lax.rem(me + wide - step, wide))

    def first_hop(chunk, step, to_pair, receiving=False):
        owner = (pair if to_pair else across) if receiving else panel
        dst = block_at(chunk, step, owner)
        src = mine(me, chunk) if step == 0 else block_at(chunk, step, panel)
        send, recv = (pair_send, pair_recv) if to_pair else (x_send, x_recv)
        return remote(src, dst, send.at[chunk, step], recv.at[chunk, step],
                      {"narrow": pair if to_pair else across})

    def second_hop(chunk, step, receiving=False):
        block = block_at(chunk, step, across_pair if receiving else across)
        return remote(block, block, last_send.at[chunk, step], last_recv.at[chunk, step],
                      {"narrow": pair})

    def begin(chunk, carry):
        first_hop(chunk, 0, False).start()
        for step in ORDER:
            along(chunk, step).start()
        first_hop(chunk, 0, True).start()
        pltpu.make_async_copy(mine(me, chunk), spot(chunk, panel, me), local_sem.at[chunk]).start()
        return carry

    def onward(chunk, carry):
        for step in range(1, wide):
            arriving(chunk, step).wait_recv()
            first_hop(chunk, step, False).start()
            first_hop(chunk, step, True).start()
        return carry

    def relay(chunk, carry):
        for step in range(wide):
            first_hop(chunk, step, False, True).wait_recv()
            second_hop(chunk, step).start()
        return carry

    def both(chunk, carry):
        onward(chunk, carry)
        relay(chunk - 1, carry)
        return carry

    def finish(chunk, carry):
        pltpu.make_async_copy(mine(me, chunk), spot(chunk, panel, me), local_sem.at[chunk]).wait()
        for step in range(wide):
            if step > 0:
                along(chunk, step).wait_send()
            first_hop(chunk, step, False).wait_send()
            first_hop(chunk, step, True).wait_send()
            first_hop(chunk, step, True, True).wait_recv()
            second_hop(chunk, step).wait_send()
            second_hop(chunk, step, True).wait_recv()
        return carry

    def transform(row_chunk, carry):
        tables = (first_ref, twist_ref, last_ref)
        dft_chunk((x0_ref, x1_ref), row_chunk, tables, flip, spectra)
        return lax.fori_loop(row_chunk * GROUPS, (row_chunk + 1) * GROUPS, begin, carry)

    lax.fori_loop(0, row_chunks, transform, 0)
    onward(0, 0)
    lax.fori_loop(1, chunks, both, 0)
    relay(chunks - 1, 0)
    lax.fori_loop(0, chunks, finish, 0)


def move(blocks, frame_len, wide, narrow, bins):
    first, twist, last = dft_tables(frame_len)
    rows, side = blocks[0].shape[0], FACTOR_A
    row_chunks = rows // ROWS
    table = pltpu.SemaphoreType.DMA((row_chunks * GROUPS, wide))
    return pl.pallas_call(
        functools.partial(move_kernel, wide),
        in_specs=[pl.BlockSpec(memory_space=pltpu.VMEM)] * 5,
        out_specs=pl.BlockSpec(memory_space=pl.ANY),
        out_shape=jax.ShapeDtypeStruct((bins, 2, narrow * wide * rows, 2 * side), jnp.bfloat16),
        scratch_shapes=[
            pltpu.VMEM((2, ROWS * side, side), jnp.float32),
            pltpu.VMEM((row_chunks, wide, bins, 2, ROWS, 2 * side), jnp.bfloat16),
            pltpu.SemaphoreType.DMA((row_chunks * GROUPS,)),
        ]
        + [table] * 8,
        compiler_params=pltpu.CompilerParams(
            collective_id=0, has_side_effects=True, vmem_limit_bytes=32 * 2**20
        ),
    )(*blocks, jnp.asarray(first), jnp.asarray(twist), jnp.asarray(last))


def filter_rows(voltages, fir_coeffs, spectrum):
    frame_len = fir_coeffs.shape[1]
    total = 0.0
    for tap_index in range(fir_coeffs.shape[0]):
        start = (spectrum + tap_index) * frame_len
        block = voltages[:, start : start + frame_len].astype(jnp.float32)
        total = total + fir_coeffs[tap_index] * block
    return total.astype(jnp.bfloat16)


def fast_body(wide, voltages, fir_coeffs, channel_keep_flags):
    tap_count, frame_len = fir_coeffs.shape
    inputs_here = voltages.shape[1]
    spectrum_count = voltages.shape[2] // frame_len - tap_count + 1
    bin_width = FACTOR_A
    local_bins = channel_keep_flags.shape[0] // bin_width
    filtered = [filter_rows(voltages[0], fir_coeffs, s) for s in range(spectrum_count)]
    blocks = [lax.optimization_barrier(x).reshape(inputs_here, FACTOR_A, FACTOR_A) for x in filtered]
    gathered = move(blocks, frame_len, wide, 4, local_bins)
    flags = channel_keep_flags.astype(jnp.bfloat16).reshape(local_bins, 1, bin_width)
    flags = jnp.concatenate([flags] * spectrum_count, axis=2)
    scale = 1.0 / (spectrum_count * bin_width)
    return correlate_bins(gathered, flags, wide * inputs_here, scale)


def solution(mesh):
    wide = mesh.shape["wide"]
    narrow = mesh.shape["narrow"]

    def body(voltages, fir_coeffs, channel_keep_flags):
        tap_count, frame_len = fir_coeffs.shape
        rows = voltages.shape[1]
        spectrum_count = voltages.shape[2] // frame_len - tap_count + 1
        fits = frame_len == FACTOR_A**2 and rows % ROWS == 0 and spectrum_count == 2
        bins_fit = channel_keep_flags.shape[0] // FACTOR_A % GROUPS == 0
        if fits and bins_fit and narrow == 4 and wide == 4:
            return fast_body(wide, voltages, fir_coeffs, channel_keep_flags)
        return plain_body(voltages, fir_coeffs, channel_keep_flags)

    placed = (P(("grp", "narrow"), "wide", None), P(), P(("grp", "wide")))
    return jax.shard_map(
        body,
        mesh=mesh,
        in_specs=placed,
        out_specs=P(("grp", "wide"), None, "narrow", None, None),
        check_vma=False,
    )
```

```python
import functools

import jax
import jax.numpy as jnp
import numpy as np
from jax import lax
from jax.experimental import pallas as pl
from jax.experimental.pallas import tpu as pltpu
from jax.sharding import PartitionSpec as P

FACTOR_A = 128


def phase_table(length, outputs, period):
    left_index = jnp.arange(length, dtype=jnp.int32)
    right_index = jnp.arange(outputs, dtype=jnp.int32)
    product = left_index[:, None] * right_index[None, :] % period
    radians = product.astype(jnp.float32) * (2.0 * jnp.pi / period)
    return (jnp.cos(radians), jnp.sin(radians))


def correlate(own_rows, incoming, norm_divisor):
    return (
        jnp.einsum("doqisc,dqmsc->doim", own_rows, incoming, preferred_element_type=jnp.float32)
        * norm_divisor
    )


def plain_body(voltages, fir_coeffs, channel_keep_flags):
    tap_count, frame_len = fir_coeffs.shape
    inputs_here = voltages.shape[1]
    spectrum_count = voltages.shape[2] // frame_len - tap_count + 1
    factor_b = frame_len // FACTOR_A
    blocks = voltages[0].reshape(inputs_here, spectrum_count + tap_count - 1, frame_len)
    filtered = jnp.zeros((inputs_here, spectrum_count, frame_len), jnp.float32)
    for tap_index in range(tap_count):
        filtered = filtered + fir_coeffs[tap_index] * blocks[
            :, tap_index : tap_index + spectrum_count
        ].astype(jnp.float32)
    rounded = lax.optimization_barrier(filtered.astype(jnp.bfloat16))
    folded = rounded.reshape(inputs_here, spectrum_count, FACTOR_A, factor_b)
    high = lax.Precision.HIGHEST
    first_cos, first_sin = phase_table(FACTOR_A, FACTOR_A, FACTOR_A)
    first_table = jnp.stack([first_cos, -first_sin], axis=1)
    table_high = first_table.astype(jnp.bfloat16)
    table_low = (first_table - table_high.astype(jnp.float32)).astype(jnp.bfloat16)
    first_pass = jnp.einsum(
        "psab,aqc->psbqc", folded, table_high, preferred_element_type=jnp.float32
    )
    first_pass = first_pass + jnp.einsum(
        "psab,aqc->psbqc", folded, table_low, preferred_element_type=jnp.float32
    )
    twist_cos, twist_sin = phase_table(factor_b, FACTOR_A, frame_len)
    real_part = first_pass[:, :, :, 0] * twist_cos + first_pass[:, :, :, 1] * twist_sin
    imag_part = first_pass[:, :, :, 1] * twist_cos - first_pass[:, :, :, 0] * twist_sin
    twisted = jnp.stack([real_part, imag_part], axis=3)
    last_cos, last_sin = phase_table(factor_b, factor_b // 2, factor_b)
    cos_rows = last_cos.T
    sin_rows = last_sin.T
    last_table = jnp.stack(
        [jnp.stack([cos_rows, sin_rows], axis=1), jnp.stack([-sin_rows, cos_rows], axis=1)], axis=1
    )
    channel_spectra = jnp.einsum("dqrb,psbrc->dqpsc", last_table, twisted, precision=high)
    channel_spectra = (channel_spectra * frame_len ** (-0.5)).astype(jnp.bfloat16)
    turned = lax.all_to_all(channel_spectra, "wide", split_axis=0, concat_axis=2, tiled=True)
    local_bins = turned.shape[0]
    bin_width = turned.shape[4]
    flag_block = channel_keep_flags.astype(jnp.bfloat16).reshape(local_bins, 1, 1, 1, bin_width)
    weighted = turned * flag_block
    rotated = jnp.stack([weighted[:, 1], -weighted[:, 0]], axis=1)
    own_rows = jnp.stack([weighted, rotated], axis=1)
    norm_divisor = 1.0 / (spectrum_count * bin_width)
    gathered = correlate(
        own_rows, lax.all_gather(turned, "narrow", axis=2, tiled=True), norm_divisor
    )
    result = gathered.astype(jnp.bfloat16)
    return result[:, :, None]


ROWS = 16
GROUPS = 4
COLUMNS = 256
ORDER = (2, 1, 3)


def split_table(table):
    high = table.astype(jnp.bfloat16)
    low = (table - high.astype(np.float64)).astype(jnp.bfloat16)
    return high, low


def dft_tables(frame_len):
    side = FACTOR_A
    index = np.arange(side)
    turn = 2.0 * np.pi * (np.outer(index, index) % side) / side
    first = np.concatenate([np.cos(turn), -np.sin(turn)], axis=0)
    first = np.concatenate(split_table(first), axis=1)
    twist = 2.0 * np.pi * np.outer(index, index) / frame_len
    twist = np.stack([np.cos(twist), np.sin(twist)]).astype(np.float32)
    last_cos, last_sin = np.cos(turn[: side // 2]), np.sin(turn[: side // 2])
    real_row = np.concatenate([last_cos, last_sin], axis=1)
    imag_row = np.concatenate([-last_sin, last_cos], axis=1)
    last = np.stack([real_row, imag_row], axis=1).reshape(side, 2 * side)
    last = last * frame_len ** (-0.5)
    last = np.concatenate(split_table(last), axis=0)
    return first, twist, last


def dft_rows(spectra_in, row, first_ref, twist_ref, last_ref, flip):
    side = FACTOR_A
    samples = jnp.concatenate([ref[row] for ref in spectra_in], axis=1)
    samples = jnp.concatenate([samples, samples], axis=0)
    first_pass = jnp.dot(first_ref[...], samples, preferred_element_type=jnp.float32)
    twisted = []
    for s in range(len(spectra_in)):
        real = first_pass[:side, s * side : (s + 1) * side]
        imag = first_pass[side:, s * side : (s + 1) * side]
        cos, sin = twist_ref[0], twist_ref[1]
        twisted.append(
            jnp.concatenate([real * cos + imag * sin, imag * cos - real * sin], axis=1)
        )
    twisted = jnp.concatenate(twisted, axis=0).astype(jnp.bfloat16)
    both = lax.dot_general(
        last_ref[...], twisted, (((1,), (1,)), ((), ())), preferred_element_type=jnp.float32
    )
    total = both[:side] + both[side:]
    start = pl.multiple_of(lax.rem(row, ROWS) * side, side)
    for s in range(len(spectra_in)):
        flip[s, pl.ds(start, side), :] = total[:, s * side : (s + 1) * side]


def dft_chunk(spectra_in, chunk, tables, flip, spectra):
    side = FACTOR_A
    _, wide, bins, parts, _, _ = spectra.shape

    def one(row, carry):
        dft_rows(spectra_in, chunk * ROWS + row, *tables, flip)
        return carry

    lax.fori_loop(0, ROWS, one, 0, unroll=4)
    for dq in range(side):
        target, bin_index, part = dq // (bins * parts), dq // parts % bins, dq % parts
        for s in range(len(spectra_in)):
            spectra[chunk, target, bin_index, part, :, s * side : (s + 1) * side] = flip[
                s, pl.ds(dq, ROWS, stride=side), :
            ].astype(jnp.bfloat16)


def correlate_kernel(scale, rows, flag_ref, all_ref, out_ref):
    start = pl.multiple_of(lax.axis_index("narrow") * rows, rows)
    flags = flag_ref[0]
    own_real = all_ref[0, 0, pl.ds(start, rows), :] * flags
    own_imag = all_ref[0, 1, pl.ds(start, rows), :] * flags
    own = jnp.concatenate(
        [
            jnp.concatenate([own_real, own_imag], axis=1),
            jnp.concatenate([own_imag, -own_real], axis=1),
        ],
        axis=0,
    )
    for first in range(0, all_ref.shape[2], COLUMNS):
        span = slice(first, first + COLUMNS)
        columns = jnp.concatenate([all_ref[0, 0, span, :], all_ref[0, 1, span, :]], axis=1)
        total = lax.dot_general(
            own, columns, (((1,), (1,)), ((), ())), preferred_element_type=jnp.float32
        )
        total = (total * scale).astype(jnp.bfloat16)
        out_ref[0, 0, 0, :, span] = total[:rows]
        out_ref[0, 1, 0, :, span] = total[rows:]


def correlate_bins(gathered, flags, rows, scale):
    bins, parts, inputs, depth = gathered.shape
    return pl.pallas_call(
        functools.partial(correlate_kernel, scale, rows),
        grid=(bins,),
        in_specs=[
            pl.BlockSpec((1, 1, depth), lambda b: (b, 0, 0)),
            pl.BlockSpec((1, parts, inputs, depth), lambda b: (b, 0, 0, 0)),
        ],
        out_specs=pl.BlockSpec((1, parts, 1, rows, inputs), lambda b: (b, 0, 0, 0, 0)),
        out_shape=jax.ShapeDtypeStruct((bins, parts, 1, rows, inputs), jnp.bfloat16),
        compiler_params=pltpu.CompilerParams(vmem_limit_bytes=20 * 2**20),
    )(flags, gathered)


def move_kernel(wide, x0_ref, x1_ref, first_ref, twist_ref, last_ref, gathered, flip, spectra,
                local_sem, z_send, z_recv, x_send, x_recv, pair_send, pair_recv, last_send,
                last_recv):
    me = lax.axis_index("wide")
    panel = lax.axis_index("narrow")
    pair = panel + 1 - 2 * lax.rem(panel, 2)
    across = lax.rem(panel + 2, 4)
    across_pair = lax.rem(pair + 2, 4)
    rows = x0_ref.shape[0]
    row_chunks = rows // ROWS
    chunks = row_chunks * GROUPS
    size = spectra.shape[2] // GROUPS

    barrier = pltpu.get_barrier_semaphore()
    peers = [{"wide": lax.rem(me + step, wide)} for step in range(1, wide)]
    peers += [{"narrow": pair}, {"narrow": across}]
    for peer in peers:
        pl.semaphore_signal(barrier, inc=1, device_id=peer, device_id_type=pl.DeviceIdType.MESH)
    pl.semaphore_wait(barrier, len(peers))

    def spot(chunk, owner, source):
        start = (owner * wide + source) * rows + chunk // GROUPS * ROWS
        group = chunk % GROUPS
        start = pl.multiple_of(start, ROWS)
        return gathered.at[pl.ds(group * size, size), :, pl.ds(start, ROWS), :]

    def mine(target, chunk):
        group = chunk % GROUPS
        return spectra.at[chunk // GROUPS, target, pl.ds(group * size, size)]

    def remote(src, dst, send, recv, peer):
        return pltpu.make_async_remote_copy(
            src_ref=src, dst_ref=dst, send_sem=send, recv_sem=recv,
            device_id=peer, device_id_type=pl.DeviceIdType.MESH,
        )

    def along(chunk, step):
        target = lax.rem(me + step, wide)
        return remote(mine(target, chunk), spot(chunk, panel, me), z_send.at[chunk, step],
                      z_recv.at[chunk, step], {"wide": target})

    def arriving(chunk, step):
        source = lax.rem(me + wide - step, wide)
        return remote(mine(me, chunk), spot(chunk, panel, source), z_send.at[chunk, step],
                      z_recv.at[chunk, step], {"wide": source})

    def block_at(chunk, step, owner):
        return spot(chunk, owner, lax.rem(me + wide - step, wide))

    def first_hop(chunk, step, to_pair, receiving=False):
        owner = (pair if to_pair else across) if receiving else panel
        dst = block_at(chunk, step, owner)
        src = mine(me, chunk) if step == 0 else block_at(chunk, step, panel)
        send, recv = (pair_send, pair_recv) if to_pair else (x_send, x_recv)
        return remote(src, dst, send.at[chunk, step], recv.at[chunk, step],
                      {"narrow": pair if to_pair else across})

    def second_hop(chunk, step, receiving=False):
        block = block_at(chunk, step, across_pair if receiving else across)
        return remote(block, block, last_send.at[chunk, step], last_recv.at[chunk, step],
                      {"narrow": pair})

    def begin(chunk, carry):
        first_hop(chunk, 0, False).start()
        for step in ORDER:
            along(chunk, step).start()
        first_hop(chunk, 0, True).start()
        pltpu.make_async_copy(mine(me, chunk), spot(chunk, panel, me), local_sem.at[chunk]).start()
        return carry

    def onward(chunk, carry):
        for step in range(1, wide):
            arriving(chunk, step).wait_recv()
            first_hop(chunk, step, False).start()
            first_hop(chunk, step, True).start()
        return carry

    def relay(chunk, carry):
        for step in range(wide):
            first_hop(chunk, step, False, True).wait_recv()
            second_hop(chunk, step).start()
        return carry

    def both(chunk, carry):
        onward(chunk, carry)
        relay(chunk - 1, carry)
        return carry

    def finish(chunk, carry):
        pltpu.make_async_copy(mine(me, chunk), spot(chunk, panel, me), local_sem.at[chunk]).wait()
        for step in range(wide):
            if step > 0:
                along(chunk, step).wait_send()
            first_hop(chunk, step, False).wait_send()
            first_hop(chunk, step, True).wait_send()
            first_hop(chunk, step, True, True).wait_recv()
            second_hop(chunk, step).wait_send()
            second_hop(chunk, step, True).wait_recv()
        return carry

    def transform(row_chunk, carry):
        tables = (first_ref, twist_ref, last_ref)
        dft_chunk((x0_ref, x1_ref), row_chunk, tables, flip, spectra)
        return lax.fori_loop(row_chunk * GROUPS, (row_chunk + 1) * GROUPS, begin, carry)

    lax.fori_loop(0, row_chunks, transform, 0)
    onward(0, 0)
    lax.fori_loop(1, chunks, both, 0)
    relay(chunks - 1, 0)
    lax.fori_loop(0, chunks, finish, 0)


def move(blocks, frame_len, wide, narrow, bins):
    first, twist, last = dft_tables(frame_len)
    rows, side = blocks[0].shape[0], FACTOR_A
    row_chunks = rows // ROWS
    table = pltpu.SemaphoreType.DMA((row_chunks * GROUPS, wide))
    return pl.pallas_call(
        functools.partial(move_kernel, wide),
        in_specs=[pl.BlockSpec(memory_space=pltpu.VMEM)] * 5,
        out_specs=pl.BlockSpec(memory_space=pl.ANY),
        out_shape=jax.ShapeDtypeStruct((bins, 2, narrow * wide * rows, 2 * side), jnp.bfloat16),
        scratch_shapes=[
            pltpu.VMEM((2, ROWS * side, side), jnp.float32),
            pltpu.VMEM((row_chunks, wide, bins, 2, ROWS, 2 * side), jnp.bfloat16),
            pltpu.SemaphoreType.DMA((row_chunks * GROUPS,)),
        ]
        + [table] * 8,
        compiler_params=pltpu.CompilerParams(
            collective_id=0, has_side_effects=True, vmem_limit_bytes=32 * 2**20
        ),
    )(*blocks, jnp.asarray(first), jnp.asarray(twist), jnp.asarray(last))


def filter_rows(voltages, fir_coeffs, spectrum):
    frame_len = fir_coeffs.shape[1]
    total = 0.0
    for tap_index in range(fir_coeffs.shape[0]):
        start = (spectrum + tap_index) * frame_len
        block = voltages[:, start : start + frame_len].astype(jnp.float32)
        total = total + fir_coeffs[tap_index] * block
    return total.astype(jnp.bfloat16)


def fast_body(wide, voltages, fir_coeffs, channel_keep_flags):
    tap_count, frame_len = fir_coeffs.shape
    inputs_here = voltages.shape[1]
    spectrum_count = voltages.shape[2] // frame_len - tap_count + 1
    bin_width = FACTOR_A
    local_bins = channel_keep_flags.shape[0] // bin_width
    filtered = [filter_rows(voltages[0], fir_coeffs, s) for s in range(spectrum_count)]
    blocks = [lax.optimization_barrier(x).reshape(inputs_here, FACTOR_A, FACTOR_A) for x in filtered]
    gathered = move(blocks, frame_len, wide, 4, local_bins)
    flags = channel_keep_flags.astype(jnp.bfloat16).reshape(local_bins, 1, bin_width)
    flags = jnp.concatenate([flags] * spectrum_count, axis=2)
    scale = 1.0 / (spectrum_count * bin_width)
    return correlate_bins(gathered, flags, wide * inputs_here, scale)


def solution(mesh):
    wide = mesh.shape["wide"]
    narrow = mesh.shape["narrow"]

    def body(voltages, fir_coeffs, channel_keep_flags):
        tap_count, frame_len = fir_coeffs.shape
        rows = voltages.shape[1]
        spectrum_count = voltages.shape[2] // frame_len - tap_count + 1
        fits = frame_len == FACTOR_A**2 and rows % ROWS == 0 and spectrum_count == 2
        bins_fit = channel_keep_flags.shape[0] // FACTOR_A % GROUPS == 0
        if fits and bins_fit and narrow == 4 and wide == 4:
            return fast_body(wide, voltages, fir_coeffs, channel_keep_flags)
        return plain_body(voltages, fir_coeffs, channel_keep_flags)

    placed = (P(("grp", "narrow"), "wide", None), P(), P(("grp", "wide")))
    return jax.shard_map(
        body,
        mesh=mesh,
        in_specs=placed,
        out_specs=P(("grp", "wide"), None, "narrow", None, None),
        check_vma=False,
    )
```

```python
import functools

import jax
import jax.numpy as jnp
import numpy as np
from jax import lax
from jax.experimental import pallas as pl
from jax.experimental.pallas import tpu as pltpu
from jax.sharding import PartitionSpec as P

FACTOR_A = 128


def phase_table(length, outputs, period):
    left_index = jnp.arange(length, dtype=jnp.int32)
    right_index = jnp.arange(outputs, dtype=jnp.int32)
    product = left_index[:, None] * right_index[None, :] % period
    radians = product.astype(jnp.float32) * (2.0 * jnp.pi / period)
    return (jnp.cos(radians), jnp.sin(radians))


def correlate(own_rows, incoming, norm_divisor):
    return (
        jnp.einsum("doqisc,dqmsc->doim", own_rows, incoming, preferred_element_type=jnp.float32)
        * norm_divisor
    )


def plain_body(voltages, fir_coeffs, channel_keep_flags):
    tap_count, frame_len = fir_coeffs.shape
    inputs_here = voltages.shape[1]
    spectrum_count = voltages.shape[2] // frame_len - tap_count + 1
    factor_b = frame_len // FACTOR_A
    blocks = voltages[0].reshape(inputs_here, spectrum_count + tap_count - 1, frame_len)
    filtered = jnp.zeros((inputs_here, spectrum_count, frame_len), jnp.float32)
    for tap_index in range(tap_count):
        filtered = filtered + fir_coeffs[tap_index] * blocks[
            :, tap_index : tap_index + spectrum_count
        ].astype(jnp.float32)
    rounded = lax.optimization_barrier(filtered.astype(jnp.bfloat16))
    folded = rounded.reshape(inputs_here, spectrum_count, FACTOR_A, factor_b)
    high = lax.Precision.HIGHEST
    first_cos, first_sin = phase_table(FACTOR_A, FACTOR_A, FACTOR_A)
    first_table = jnp.stack([first_cos, -first_sin], axis=1)
    table_high = first_table.astype(jnp.bfloat16)
    table_low = (first_table - table_high.astype(jnp.float32)).astype(jnp.bfloat16)
    first_pass = jnp.einsum(
        "psab,aqc->psbqc", folded, table_high, preferred_element_type=jnp.float32
    )
    first_pass = first_pass + jnp.einsum(
        "psab,aqc->psbqc", folded, table_low, preferred_element_type=jnp.float32
    )
    twist_cos, twist_sin = phase_table(factor_b, FACTOR_A, frame_len)
    real_part = first_pass[:, :, :, 0] * twist_cos + first_pass[:, :, :, 1] * twist_sin
    imag_part = first_pass[:, :, :, 1] * twist_cos - first_pass[:, :, :, 0] * twist_sin
    twisted = jnp.stack([real_part, imag_part], axis=3)
    last_cos, last_sin = phase_table(factor_b, factor_b // 2, factor_b)
    cos_rows = last_cos.T
    sin_rows = last_sin.T
    last_table = jnp.stack(
        [jnp.stack([cos_rows, sin_rows], axis=1), jnp.stack([-sin_rows, cos_rows], axis=1)], axis=1
    )
    channel_spectra = jnp.einsum("dqrb,psbrc->dqpsc", last_table, twisted, precision=high)
    channel_spectra = (channel_spectra * frame_len ** (-0.5)).astype(jnp.bfloat16)
    turned = lax.all_to_all(channel_spectra, "wide", split_axis=0, concat_axis=2, tiled=True)
    local_bins = turned.shape[0]
    bin_width = turned.shape[4]
    flag_block = channel_keep_flags.astype(jnp.bfloat16).reshape(local_bins, 1, 1, 1, bin_width)
    weighted = turned * flag_block
    rotated = jnp.stack([weighted[:, 1], -weighted[:, 0]], axis=1)
    own_rows = jnp.stack([weighted, rotated], axis=1)
    norm_divisor = 1.0 / (spectrum_count * bin_width)
    gathered = correlate(
        own_rows, lax.all_gather(turned, "narrow", axis=2, tiled=True), norm_divisor
    )
    result = gathered.astype(jnp.bfloat16)
    return result[:, :, None]


ROWS = 16
GROUPS = 4
COLUMNS = 256


def split_table(table):
    high = table.astype(jnp.bfloat16)
    low = (table - high.astype(np.float64)).astype(jnp.bfloat16)
    return high, low


def dft_tables(frame_len):
    side = FACTOR_A
    index = np.arange(side)
    turn = 2.0 * np.pi * (np.outer(index, index) % side) / side
    first = np.concatenate([np.cos(turn), -np.sin(turn)], axis=0)
    first = np.concatenate(split_table(first), axis=1)
    twist = 2.0 * np.pi * np.outer(index, index) / frame_len
    twist = np.stack([np.cos(twist), np.sin(twist)]).astype(np.float32)
    last_cos, last_sin = np.cos(turn[: side // 2]), np.sin(turn[: side // 2])
    real_row = np.concatenate([last_cos, last_sin], axis=1)
    imag_row = np.concatenate([-last_sin, last_cos], axis=1)
    last = np.stack([real_row, imag_row], axis=1).reshape(side, 2 * side)
    last = last * frame_len ** (-0.5)
    last = np.concatenate(split_table(last), axis=0)
    return first, twist, last


def dft_rows(spectra_in, row, first_ref, twist_ref, last_ref, flip):
    side = FACTOR_A
    samples = jnp.concatenate([ref[row] for ref in spectra_in], axis=1)
    samples = jnp.concatenate([samples, samples], axis=0)
    first_pass = jnp.dot(first_ref[...], samples, preferred_element_type=jnp.float32)
    twisted = []
    for s in range(len(spectra_in)):
        real = first_pass[:side, s * side : (s + 1) * side]
        imag = first_pass[side:, s * side : (s + 1) * side]
        cos, sin = twist_ref[0], twist_ref[1]
        twisted.append(
            jnp.concatenate([real * cos + imag * sin, imag * cos - real * sin], axis=1)
        )
    twisted = jnp.concatenate(twisted, axis=0).astype(jnp.bfloat16)
    both = lax.dot_general(
        last_ref[...], twisted, (((1,), (1,)), ((), ())), preferred_element_type=jnp.float32
    )
    total = both[:side] + both[side:]
    start = pl.multiple_of(lax.rem(row, ROWS) * side, side)
    for s in range(len(spectra_in)):
        flip[s, pl.ds(start, side), :] = total[:, s * side : (s + 1) * side]


def dft_chunk(spectra_in, chunk, tables, flip, spectra):
    side = FACTOR_A
    _, wide, bins, parts, _, _ = spectra.shape

    def one(row, carry):
        dft_rows(spectra_in, chunk * ROWS + row, *tables, flip)
        return carry

    lax.fori_loop(0, ROWS, one, 0, unroll=4)
    for dq in range(side):
        target, bin_index, part = dq // (bins * parts), dq // parts % bins, dq % parts
        for s in range(len(spectra_in)):
            spectra[chunk, target, bin_index, part, :, s * side : (s + 1) * side] = flip[
                s, pl.ds(dq, ROWS, stride=side), :
            ].astype(jnp.bfloat16)


def correlate_kernel(scale, rows, flag_ref, all_ref, out_ref):
    start = pl.multiple_of(lax.axis_index("narrow") * rows, rows)
    flags = flag_ref[0]
    own_real = all_ref[0, 0, pl.ds(start, rows), :] * flags
    own_imag = all_ref[0, 1, pl.ds(start, rows), :] * flags
    own = jnp.concatenate(
        [
            jnp.concatenate([own_real, own_imag], axis=1),
            jnp.concatenate([own_imag, -own_real], axis=1),
        ],
        axis=0,
    )
    for first in range(0, all_ref.shape[2], COLUMNS):
        span = slice(first, first + COLUMNS)
        columns = jnp.concatenate([all_ref[0, 0, span, :], all_ref[0, 1, span, :]], axis=1)
        total = lax.dot_general(
            own, columns, (((1,), (1,)), ((), ())), preferred_element_type=jnp.float32
        )
        total = (total * scale).astype(jnp.bfloat16)
        out_ref[0, 0, 0, :, span] = total[:rows]
        out_ref[0, 1, 0, :, span] = total[rows:]


def correlate_bins(gathered, flags, rows, scale):
    bins, parts, inputs, depth = gathered.shape
    return pl.pallas_call(
        functools.partial(correlate_kernel, scale, rows),
        grid=(bins,),
        in_specs=[
            pl.BlockSpec((1, 1, depth), lambda b: (b, 0, 0)),
            pl.BlockSpec((1, parts, inputs, depth), lambda b: (b, 0, 0, 0)),
        ],
        out_specs=pl.BlockSpec((1, parts, 1, rows, inputs), lambda b: (b, 0, 0, 0, 0)),
        out_shape=jax.ShapeDtypeStruct((bins, parts, 1, rows, inputs), jnp.bfloat16),
        compiler_params=pltpu.CompilerParams(vmem_limit_bytes=20 * 2**20),
    )(flags, gathered)


def move_kernel(wide, x0_ref, x1_ref, first_ref, twist_ref, last_ref, gathered, flip, spectra,
                local_sem, z_send, z_recv, x_send, x_recv, pair_send, pair_recv, last_send,
                last_recv):
    me = lax.axis_index("wide")
    panel = lax.axis_index("narrow")
    pair = panel + 1 - 2 * lax.rem(panel, 2)
    across = lax.rem(panel + 2, 4)
    across_pair = lax.rem(pair + 2, 4)
    rows = x0_ref.shape[0]
    row_chunks = rows // ROWS
    chunks = row_chunks * GROUPS
    size = spectra.shape[2] // GROUPS

    barrier = pltpu.get_barrier_semaphore()
    peers = [{"wide": lax.rem(me + step, wide)} for step in range(1, wide)]
    peers += [{"narrow": pair}, {"narrow": across}]
    for peer in peers:
        pl.semaphore_signal(barrier, inc=1, device_id=peer, device_id_type=pl.DeviceIdType.MESH)
    pl.semaphore_wait(barrier, len(peers))

    def spot(chunk, owner, source):
        start = (owner * wide + source) * rows + chunk // GROUPS * ROWS
        group = chunk % GROUPS
        start = pl.multiple_of(start, ROWS)
        return gathered.at[pl.ds(group * size, size), :, pl.ds(start, ROWS), :]

    def mine(target, chunk):
        group = chunk % GROUPS
        return spectra.at[chunk // GROUPS, target, pl.ds(group * size, size)]

    def remote(src, dst, send, recv, peer):
        return pltpu.make_async_remote_copy(
            src_ref=src, dst_ref=dst, send_sem=send, recv_sem=recv,
            device_id=peer, device_id_type=pl.DeviceIdType.MESH,
        )

    def along(chunk, step):
        target = lax.rem(me + step, wide)
        return remote(mine(target, chunk), spot(chunk, panel, me), z_send.at[chunk, step],
                      z_recv.at[chunk, step], {"wide": target})

    def arriving(chunk, step):
        source = lax.rem(me + wide - step, wide)
        return remote(mine(me, chunk), spot(chunk, panel, source), z_send.at[chunk, step],
                      z_recv.at[chunk, step], {"wide": source})

    def block_at(chunk, step, owner):
        return spot(chunk, owner, lax.rem(me + wide - step, wide))

    def first_hop(chunk, step, to_pair, receiving=False):
        owner = (pair if to_pair else across) if receiving else panel
        dst = block_at(chunk, step, owner)
        src = mine(me, chunk) if step == 0 else block_at(chunk, step, panel)
        send, recv = (pair_send, pair_recv) if to_pair else (x_send, x_recv)
        return remote(src, dst, send.at[chunk, step], recv.at[chunk, step],
                      {"narrow": pair if to_pair else across})

    def second_hop(chunk, step, receiving=False):
        block = block_at(chunk, step, across_pair if receiving else across)
        return remote(block, block, last_send.at[chunk, step], last_recv.at[chunk, step],
                      {"narrow": pair})

    def begin(chunk, carry):
        first_hop(chunk, 0, False).start()
        near = 1 + 2 * lax.rem(me, 2)
        for step in (2, 4 - near, near):
            along(chunk, step).start()
        first_hop(chunk, 0, True).start()
        pltpu.make_async_copy(mine(me, chunk), spot(chunk, panel, me), local_sem.at[chunk]).start()
        return carry

    def onward(chunk, carry):
        for step in range(1, wide):
            arriving(chunk, step).wait_recv()
            first_hop(chunk, step, False).start()
            first_hop(chunk, step, True).start()
        return carry

    def relay(chunk, carry):
        for step in range(wide):
            first_hop(chunk, step, False, True).wait_recv()
            second_hop(chunk, step).start()
        return carry

    def both(chunk, carry):
        onward(chunk, carry)
        relay(chunk - 1, carry)
        return carry

    def finish(chunk, carry):
        pltpu.make_async_copy(mine(me, chunk), spot(chunk, panel, me), local_sem.at[chunk]).wait()
        for step in range(wide):
            if step > 0:
                along(chunk, step).wait_send()
            first_hop(chunk, step, False).wait_send()
            first_hop(chunk, step, True).wait_send()
            first_hop(chunk, step, True, True).wait_recv()
            second_hop(chunk, step).wait_send()
            second_hop(chunk, step, True).wait_recv()
        return carry

    def transform(row_chunk, carry):
        tables = (first_ref, twist_ref, last_ref)
        dft_chunk((x0_ref, x1_ref), row_chunk, tables, flip, spectra)
        return lax.fori_loop(row_chunk * GROUPS, (row_chunk + 1) * GROUPS, begin, carry)

    lax.fori_loop(0, row_chunks, transform, 0)
    onward(0, 0)
    lax.fori_loop(1, chunks, both, 0)
    relay(chunks - 1, 0)
    lax.fori_loop(0, chunks, finish, 0)


def move(blocks, frame_len, wide, narrow, bins):
    first, twist, last = dft_tables(frame_len)
    rows, side = blocks[0].shape[0], FACTOR_A
    row_chunks = rows // ROWS
    table = pltpu.SemaphoreType.DMA((row_chunks * GROUPS, wide))
    return pl.pallas_call(
        functools.partial(move_kernel, wide),
        in_specs=[pl.BlockSpec(memory_space=pltpu.VMEM)] * 5,
        out_specs=pl.BlockSpec(memory_space=pl.ANY),
        out_shape=jax.ShapeDtypeStruct((bins, 2, narrow * wide * rows, 2 * side), jnp.bfloat16),
        scratch_shapes=[
            pltpu.VMEM((2, ROWS * side, side), jnp.float32),
            pltpu.VMEM((row_chunks, wide, bins, 2, ROWS, 2 * side), jnp.bfloat16),
            pltpu.SemaphoreType.DMA((row_chunks * GROUPS,)),
        ]
        + [table] * 8,
        compiler_params=pltpu.CompilerParams(
            collective_id=0, has_side_effects=True, vmem_limit_bytes=32 * 2**20
        ),
    )(*blocks, jnp.asarray(first), jnp.asarray(twist), jnp.asarray(last))


def filter_rows(voltages, fir_coeffs, spectrum):
    frame_len = fir_coeffs.shape[1]
    total = 0.0
    for tap_index in range(fir_coeffs.shape[0]):
        start = (spectrum + tap_index) * frame_len
        block = voltages[:, start : start + frame_len].astype(jnp.float32)
        total = total + fir_coeffs[tap_index] * block
    return total.astype(jnp.bfloat16)


def fast_body(wide, voltages, fir_coeffs, channel_keep_flags):
    tap_count, frame_len = fir_coeffs.shape
    inputs_here = voltages.shape[1]
    spectrum_count = voltages.shape[2] // frame_len - tap_count + 1
    bin_width = FACTOR_A
    local_bins = channel_keep_flags.shape[0] // bin_width
    filtered = [filter_rows(voltages[0], fir_coeffs, s) for s in range(spectrum_count)]
    blocks = [lax.optimization_barrier(x).reshape(inputs_here, FACTOR_A, FACTOR_A) for x in filtered]
    gathered = move(blocks, frame_len, wide, 4, local_bins)
    flags = channel_keep_flags.astype(jnp.bfloat16).reshape(local_bins, 1, bin_width)
    flags = jnp.concatenate([flags] * spectrum_count, axis=2)
    scale = 1.0 / (spectrum_count * bin_width)
    return correlate_bins(gathered, flags, wide * inputs_here, scale)


def solution(mesh):
    wide = mesh.shape["wide"]
    narrow = mesh.shape["narrow"]

    def body(voltages, fir_coeffs, channel_keep_flags):
        tap_count, frame_len = fir_coeffs.shape
        rows = voltages.shape[1]
        spectrum_count = voltages.shape[2] // frame_len - tap_count + 1
        fits = frame_len == FACTOR_A**2 and rows % ROWS == 0 and spectrum_count == 2
        bins_fit = channel_keep_flags.shape[0] // FACTOR_A % GROUPS == 0
        if fits and bins_fit and narrow == 4 and wide == 4:
            return fast_body(wide, voltages, fir_coeffs, channel_keep_flags)
        return plain_body(voltages, fir_coeffs, channel_keep_flags)

    placed = (P(("grp", "narrow"), "wide", None), P(), P(("grp", "wide")))
    return jax.shard_map(
        body,
        mesh=mesh,
        in_specs=placed,
        out_specs=P(("grp", "wide"), None, "narrow", None, None),
        check_vma=False,
    )
```

```python
import functools

import jax
import jax.numpy as jnp
import numpy as np
from jax import lax
from jax.experimental import pallas as pl
from jax.experimental.pallas import tpu as pltpu
from jax.sharding import PartitionSpec as P

FACTOR_A = 128


def phase_table(length, outputs, period):
    left_index = jnp.arange(length, dtype=jnp.int32)
    right_index = jnp.arange(outputs, dtype=jnp.int32)
    product = left_index[:, None] * right_index[None, :] % period
    radians = product.astype(jnp.float32) * (2.0 * jnp.pi / period)
    return (jnp.cos(radians), jnp.sin(radians))


def correlate(own_rows, incoming, norm_divisor):
    return (
        jnp.einsum("doqisc,dqmsc->doim", own_rows, incoming, preferred_element_type=jnp.float32)
        * norm_divisor
    )


def plain_body(voltages, fir_coeffs, channel_keep_flags):
    tap_count, frame_len = fir_coeffs.shape
    inputs_here = voltages.shape[1]
    spectrum_count = voltages.shape[2] // frame_len - tap_count + 1
    factor_b = frame_len // FACTOR_A
    blocks = voltages[0].reshape(inputs_here, spectrum_count + tap_count - 1, frame_len)
    filtered = jnp.zeros((inputs_here, spectrum_count, frame_len), jnp.float32)
    for tap_index in range(tap_count):
        filtered = filtered + fir_coeffs[tap_index] * blocks[
            :, tap_index : tap_index + spectrum_count
        ].astype(jnp.float32)
    rounded = lax.optimization_barrier(filtered.astype(jnp.bfloat16))
    folded = rounded.reshape(inputs_here, spectrum_count, FACTOR_A, factor_b)
    high = lax.Precision.HIGHEST
    first_cos, first_sin = phase_table(FACTOR_A, FACTOR_A, FACTOR_A)
    first_table = jnp.stack([first_cos, -first_sin], axis=1)
    table_high = first_table.astype(jnp.bfloat16)
    table_low = (first_table - table_high.astype(jnp.float32)).astype(jnp.bfloat16)
    first_pass = jnp.einsum(
        "psab,aqc->psbqc", folded, table_high, preferred_element_type=jnp.float32
    )
    first_pass = first_pass + jnp.einsum(
        "psab,aqc->psbqc", folded, table_low, preferred_element_type=jnp.float32
    )
    twist_cos, twist_sin = phase_table(factor_b, FACTOR_A, frame_len)
    real_part = first_pass[:, :, :, 0] * twist_cos + first_pass[:, :, :, 1] * twist_sin
    imag_part = first_pass[:, :, :, 1] * twist_cos - first_pass[:, :, :, 0] * twist_sin
    twisted = jnp.stack([real_part, imag_part], axis=3)
    last_cos, last_sin = phase_table(factor_b, factor_b // 2, factor_b)
    cos_rows = last_cos.T
    sin_rows = last_sin.T
    last_table = jnp.stack(
        [jnp.stack([cos_rows, sin_rows], axis=1), jnp.stack([-sin_rows, cos_rows], axis=1)], axis=1
    )
    channel_spectra = jnp.einsum("dqrb,psbrc->dqpsc", last_table, twisted, precision=high)
    channel_spectra = (channel_spectra * frame_len ** (-0.5)).astype(jnp.bfloat16)
    turned = lax.all_to_all(channel_spectra, "wide", split_axis=0, concat_axis=2, tiled=True)
    local_bins = turned.shape[0]
    bin_width = turned.shape[4]
    flag_block = channel_keep_flags.astype(jnp.bfloat16).reshape(local_bins, 1, 1, 1, bin_width)
    weighted = turned * flag_block
    rotated = jnp.stack([weighted[:, 1], -weighted[:, 0]], axis=1)
    own_rows = jnp.stack([weighted, rotated], axis=1)
    norm_divisor = 1.0 / (spectrum_count * bin_width)
    gathered = correlate(
        own_rows, lax.all_gather(turned, "narrow", axis=2, tiled=True), norm_divisor
    )
    result = gathered.astype(jnp.bfloat16)
    return result[:, :, None]


ROWS = 16
GROUPS = 2
COLUMNS = 256


def split_table(table):
    high = table.astype(jnp.bfloat16)
    low = (table - high.astype(np.float64)).astype(jnp.bfloat16)
    return high, low


def dft_tables(frame_len):
    side = FACTOR_A
    index = np.arange(side)
    turn = 2.0 * np.pi * (np.outer(index, index) % side) / side
    first = np.concatenate([np.cos(turn), -np.sin(turn)], axis=0)
    first = np.concatenate(split_table(first), axis=1)
    twist = 2.0 * np.pi * np.outer(index, index) / frame_len
    twist = np.stack([np.cos(twist), np.sin(twist)]).astype(np.float32)
    last_cos, last_sin = np.cos(turn[: side // 2]), np.sin(turn[: side // 2])
    real_row = np.concatenate([last_cos, last_sin], axis=1)
    imag_row = np.concatenate([-last_sin, last_cos], axis=1)
    last = np.stack([real_row, imag_row], axis=1).reshape(side, 2 * side)
    last = last * frame_len ** (-0.5)
    last = np.concatenate(split_table(last), axis=0)
    return first, twist, last


def dft_rows(spectra_in, row, first_ref, twist_ref, last_ref, flip):
    side = FACTOR_A
    samples = jnp.concatenate([ref[row] for ref in spectra_in], axis=1)
    samples = jnp.concatenate([samples, samples], axis=0)
    first_pass = jnp.dot(first_ref[...], samples, preferred_element_type=jnp.float32)
    twisted = []
    for s in range(len(spectra_in)):
        real = first_pass[:side, s * side : (s + 1) * side]
        imag = first_pass[side:, s * side : (s + 1) * side]
        cos, sin = twist_ref[0], twist_ref[1]
        twisted.append(
            jnp.concatenate([real * cos + imag * sin, imag * cos - real * sin], axis=1)
        )
    twisted = jnp.concatenate(twisted, axis=0).astype(jnp.bfloat16)
    both = lax.dot_general(
        last_ref[...], twisted, (((1,), (1,)), ((), ())), preferred_element_type=jnp.float32
    )
    total = both[:side] + both[side:]
    start = pl.multiple_of(lax.rem(row, ROWS) * side, side)
    for s in range(len(spectra_in)):
        flip[s, pl.ds(start, side), :] = total[:, s * side : (s + 1) * side]


def dft_chunk(spectra_in, chunk, tables, flip, spectra):
    side = FACTOR_A
    _, wide, bins, parts, _, _ = spectra.shape

    def one(row, carry):
        dft_rows(spectra_in, chunk * ROWS + row, *tables, flip)
        return carry

    lax.fori_loop(0, ROWS, one, 0, unroll=4)
    for dq in range(side):
        target, bin_index, part = dq // (bins * parts), dq // parts % bins, dq % parts
        for s in range(len(spectra_in)):
            spectra[chunk, target, bin_index, part, :, s * side : (s + 1) * side] = flip[
                s, pl.ds(dq, ROWS, stride=side), :
            ].astype(jnp.bfloat16)


def correlate_kernel(scale, rows, flag_ref, all_ref, out_ref):
    start = pl.multiple_of(lax.axis_index("narrow") * rows, rows)
    flags = flag_ref[0]
    own_real = all_ref[0, 0, pl.ds(start, rows), :] * flags
    own_imag = all_ref[0, 1, pl.ds(start, rows), :] * flags
    own = jnp.concatenate(
        [
            jnp.concatenate([own_real, own_imag], axis=1),
            jnp.concatenate([own_imag, -own_real], axis=1),
        ],
        axis=0,
    )
    for first in range(0, all_ref.shape[2], COLUMNS):
        span = slice(first, first + COLUMNS)
        columns = jnp.concatenate([all_ref[0, 0, span, :], all_ref[0, 1, span, :]], axis=1)
        total = lax.dot_general(
            own, columns, (((1,), (1,)), ((), ())), preferred_element_type=jnp.float32
        )
        total = (total * scale).astype(jnp.bfloat16)
        out_ref[0, 0, 0, :, span] = total[:rows]
        out_ref[0, 1, 0, :, span] = total[rows:]


def correlate_bins(gathered, flags, rows, scale):
    bins, parts, inputs, depth = gathered.shape
    return pl.pallas_call(
        functools.partial(correlate_kernel, scale, rows),
        grid=(bins,),
        in_specs=[
            pl.BlockSpec((1, 1, depth), lambda b: (b, 0, 0)),
            pl.BlockSpec((1, parts, inputs, depth), lambda b: (b, 0, 0, 0)),
        ],
        out_specs=pl.BlockSpec((1, parts, 1, rows, inputs), lambda b: (b, 0, 0, 0, 0)),
        out_shape=jax.ShapeDtypeStruct((bins, parts, 1, rows, inputs), jnp.bfloat16),
        compiler_params=pltpu.CompilerParams(vmem_limit_bytes=20 * 2**20),
    )(flags, gathered)


def move_kernel(wide, x0_ref, x1_ref, first_ref, twist_ref, last_ref, gathered, flip, spectra,
                local_sem, z_send, z_recv, x_send, x_recv, pair_send, pair_recv, last_send,
                last_recv):
    me = lax.axis_index("wide")
    panel = lax.axis_index("narrow")
    pair = panel + 1 - 2 * lax.rem(panel, 2)
    across = lax.rem(panel + 2, 4)
    across_pair = lax.rem(pair + 2, 4)
    rows = x0_ref.shape[0]
    row_chunks = rows // ROWS
    chunks = row_chunks * GROUPS
    size = spectra.shape[2] // GROUPS

    barrier = pltpu.get_barrier_semaphore()
    peers = [{"wide": lax.rem(me + step, wide)} for step in range(1, wide)]
    peers += [{"narrow": pair}, {"narrow": across}]
    for peer in peers:
        pl.semaphore_signal(barrier, inc=1, device_id=peer, device_id_type=pl.DeviceIdType.MESH)
    pl.semaphore_wait(barrier, len(peers))

    def spot(chunk, owner, source):
        start = (owner * wide + source) * rows + chunk // GROUPS * ROWS
        group = chunk % GROUPS
        start = pl.multiple_of(start, ROWS)
        return gathered.at[pl.ds(group * size, size), :, pl.ds(start, ROWS), :]

    def mine(target, chunk):
        group = chunk % GROUPS
        return spectra.at[chunk // GROUPS, target, pl.ds(group * size, size)]

    def remote(src, dst, send, recv, peer):
        return pltpu.make_async_remote_copy(
            src_ref=src, dst_ref=dst, send_sem=send, recv_sem=recv,
            device_id=peer, device_id_type=pl.DeviceIdType.MESH,
        )

    def along(chunk, step):
        target = lax.rem(me + step, wide)
        return remote(mine(target, chunk), spot(chunk, panel, me), z_send.at[chunk, step],
                      z_recv.at[chunk, step], {"wide": target})

    def arriving(chunk, step):
        source = lax.rem(me + wide - step, wide)
        return remote(mine(me, chunk), spot(chunk, panel, source), z_send.at[chunk, step],
                      z_recv.at[chunk, step], {"wide": source})

    def block_at(chunk, step, owner):
        return spot(chunk, owner, lax.rem(me + wide - step, wide))

    def first_hop(chunk, step, to_pair, receiving=False):
        owner = (pair if to_pair else across) if receiving else panel
        dst = block_at(chunk, step, owner)
        src = mine(me, chunk) if step == 0 else block_at(chunk, step, panel)
        send, recv = (pair_send, pair_recv) if to_pair else (x_send, x_recv)
        return remote(src, dst, send.at[chunk, step], recv.at[chunk, step],
                      {"narrow": pair if to_pair else across})

    def second_hop(chunk, step, receiving=False):
        block = block_at(chunk, step, across_pair if receiving else across)
        return remote(block, block, last_send.at[chunk, step], last_recv.at[chunk, step],
                      {"narrow": pair})

    def begin(chunk, carry):
        first_hop(chunk, 0, False).start()
        near = 1 + 2 * lax.rem(me, 2)
        for step in (2, 4 - near, near):
            along(chunk, step).start()
        first_hop(chunk, 0, True).start()
        pltpu.make_async_copy(mine(me, chunk), spot(chunk, panel, me), local_sem.at[chunk]).start()
        return carry

    def onward(chunk, carry):
        for step in range(1, wide):
            arriving(chunk, step).wait_recv()
            first_hop(chunk, step, False).start()
            first_hop(chunk, step, True).start()
        return carry

    def relay(chunk, carry):
        for step in range(wide):
            first_hop(chunk, step, False, True).wait_recv()
            second_hop(chunk, step).start()
        return carry

    def both(chunk, carry):
        onward(chunk, carry)
        relay(chunk - 1, carry)
        return carry

    def finish(chunk, carry):
        pltpu.make_async_copy(mine(me, chunk), spot(chunk, panel, me), local_sem.at[chunk]).wait()
        for step in range(wide):
            if step > 0:
                along(chunk, step).wait_send()
            first_hop(chunk, step, False).wait_send()
            first_hop(chunk, step, True).wait_send()
            first_hop(chunk, step, True, True).wait_recv()
            second_hop(chunk, step).wait_send()
            second_hop(chunk, step, True).wait_recv()
        return carry

    def transform(row_chunk, carry):
        tables = (first_ref, twist_ref, last_ref)
        dft_chunk((x0_ref, x1_ref), row_chunk, tables, flip, spectra)
        return lax.fori_loop(row_chunk * GROUPS, (row_chunk + 1) * GROUPS, begin, carry)

    lax.fori_loop(0, row_chunks, transform, 0)
    onward(0, 0)
    lax.fori_loop(1, chunks, both, 0)
    relay(chunks - 1, 0)
    lax.fori_loop(0, chunks, finish, 0)


def move(blocks, frame_len, wide, narrow, bins):
    first, twist, last = dft_tables(frame_len)
    rows, side = blocks[0].shape[0], FACTOR_A
    row_chunks = rows // ROWS
    table = pltpu.SemaphoreType.DMA((row_chunks * GROUPS, wide))
    return pl.pallas_call(
        functools.partial(move_kernel, wide),
        in_specs=[pl.BlockSpec(memory_space=pltpu.VMEM)] * 5,
        out_specs=pl.BlockSpec(memory_space=pl.ANY),
        out_shape=jax.ShapeDtypeStruct((bins, 2, narrow * wide * rows, 2 * side), jnp.bfloat16),
        scratch_shapes=[
            pltpu.VMEM((2, ROWS * side, side), jnp.float32),
            pltpu.VMEM((row_chunks, wide, bins, 2, ROWS, 2 * side), jnp.bfloat16),
            pltpu.SemaphoreType.DMA((row_chunks * GROUPS,)),
        ]
        + [table] * 8,
        compiler_params=pltpu.CompilerParams(
            collective_id=0, has_side_effects=True, vmem_limit_bytes=32 * 2**20
        ),
    )(*blocks, jnp.asarray(first), jnp.asarray(twist), jnp.asarray(last))


def filter_rows(voltages, fir_coeffs, spectrum):
    frame_len = fir_coeffs.shape[1]
    total = 0.0
    for tap_index in range(fir_coeffs.shape[0]):
        start = (spectrum + tap_index) * frame_len
        block = voltages[:, start : start + frame_len].astype(jnp.float32)
        total = total + fir_coeffs[tap_index] * block
    return total.astype(jnp.bfloat16)


def fast_body(wide, voltages, fir_coeffs, channel_keep_flags):
    tap_count, frame_len = fir_coeffs.shape
    inputs_here = voltages.shape[1]
    spectrum_count = voltages.shape[2] // frame_len - tap_count + 1
    bin_width = FACTOR_A
    local_bins = channel_keep_flags.shape[0] // bin_width
    filtered = [filter_rows(voltages[0], fir_coeffs, s) for s in range(spectrum_count)]
    blocks = [lax.optimization_barrier(x).reshape(inputs_here, FACTOR_A, FACTOR_A) for x in filtered]
    gathered = move(blocks, frame_len, wide, 4, local_bins)
    flags = channel_keep_flags.astype(jnp.bfloat16).reshape(local_bins, 1, bin_width)
    flags = jnp.concatenate([flags] * spectrum_count, axis=2)
    scale = 1.0 / (spectrum_count * bin_width)
    return correlate_bins(gathered, flags, wide * inputs_here, scale)


def solution(mesh):
    wide = mesh.shape["wide"]
    narrow = mesh.shape["narrow"]

    def body(voltages, fir_coeffs, channel_keep_flags):
        tap_count, frame_len = fir_coeffs.shape
        rows = voltages.shape[1]
        spectrum_count = voltages.shape[2] // frame_len - tap_count + 1
        fits = frame_len == FACTOR_A**2 and rows % ROWS == 0 and spectrum_count == 2
        bins_fit = channel_keep_flags.shape[0] // FACTOR_A % GROUPS == 0
        if fits and bins_fit and narrow == 4 and wide == 4:
            return fast_body(wide, voltages, fir_coeffs, channel_keep_flags)
        return plain_body(voltages, fir_coeffs, channel_keep_flags)

    placed = (P(("grp", "narrow"), "wide", None), P(), P(("grp", "wide")))
    return jax.shard_map(
        body,
        mesh=mesh,
        in_specs=placed,
        out_specs=P(("grp", "wide"), None, "narrow", None, None),
        check_vma=False,
    )
```
